256 devices in a mesh: box: 64 (over z, y, core), col: 4 (over x).
Axes of the slice: x: 4, y: 4, z: 8, core: 2. Of those that a mesh axis runs over, the one named last changes fastest.
Arguments:
- box_points: float32 [128, 3, 512], P('box'), may hold values from 0 to 1
- proxy_directions: float32 [3, 1024], P(None, 'col'), may hold values from -1 to 1, as said below
- point_order: int32 [128, 512], P('box'), may hold values from 0 to 511, each once within a row
- neighbour_boxes: int32 [128, 8], P('box'), may hold values from 0 to 127, as said below
- neighbour_places: int32 [128, 8], P('box'), may hold values from 0 to 25
- pivot_inverse: float32 [128, 2, 256], P('box', None, 'col'), may hold values from -6 to 6
Outputs:
- interpolation: float32 [128, 2, 256, 256], P('box', None, None, 'col')
- skeleton_update: float32 [128, 2, 256, 256], P('box', None, 'col')
The draws below stay inside these ranges and needn't reach their ends.
Inputs may be any that keep to these rules, and one draw needn't show every extreme that they name: `neighbour_boxes`: box g is held by index g // 2 of the box axis. Every entry names a box of the same index or of the index just before or just after it, cyclically. Of the 16 entries of one index's boxes exactly half name boxes of that same index, never the listing box itself; a box may be listed twice in one row. `proxy_directions`: unit vectors.
All inputs are finite; a program needn't handle non-finite values.
Results may differ from the reference program's by a relative error of at most 0.0038.
Values sent between devices are 32-bit elements; how exact they have to be, the bound alone decides.
No kernel may reach another device: no remote copies, remote signals or barrier semaphores. Data moves between devices by JAX's collectives and lax.ppermute only.
A program may use at most 64 MiB of HBM per device.

```python
import math
import jax
import jax.numpy as jnp
from jax import lax

P_SIZE = 512
S = 256
PROXY = 1024
NB = 8
BOX_DEV = 2
R = 256
BOXES = 128


def draw_proxy_directions(key, part):
    samples = jax.random.normal(key, (3, PROXY), jnp.float32)
    length = jnp.sqrt(jnp.sum(samples * samples, axis=0, keepdims=True)) + 1e-06
    return samples / length


def draw_neighbour_boxes(key, part):
    device_count = BOXES // BOX_DEV
    entries = BOX_DEV * NB
    key_list = jax.random.split(jax.random.fold_in(key, 17), 4)
    places = jax.vmap(lambda one_key: jax.random.permutation(one_key, entries))(jax.random.split(key_list[0], device_count))
    side_sign = 2 * jax.random.randint(key_list[1], (device_count, entries), 0, 2) - 1
    entry_rank = jnp.arange(entries, dtype=jnp.int32)[None, :]
    own_side = entry_rank < entries // 2
    device_step = jnp.where(own_side, 0, side_sign)
    home_box = places // NB
    own_slot = (home_box + 1 + jax.random.randint(key_list[2], (device_count, entries), 0, BOX_DEV - 1)) % BOX_DEV
    far_slot = jax.random.randint(key_list[3], (device_count, entries), 0, BOX_DEV)
    chosen_slot = jnp.where(own_side, own_slot, far_slot)
    device_rank = jnp.arange(device_count, dtype=jnp.int32)[:, None]
    target = (device_rank + device_step) % device_count * BOX_DEV + chosen_slot
    neighbour_table = jnp.zeros((device_count, entries), jnp.int32).at[device_rank, places].set(target.astype(jnp.int32))
    return neighbour_table.reshape(BOXES, NB)


def place_ends(values, rng, smallest, high):
    longest = values.shape.index(max(values.shape))
    spots = []
    for shift in (0, 1):
        where = [jax.random.randint(jax.random.fold_in(rng, axis), (), 0, length) for axis, length in enumerate(values.shape)]
        where[longest] = (where[longest] + shift) % values.shape[longest]
        spots.append(tuple(where))
    return values.at[spots[0]].set(smallest).at[spots[1]].set(high)


def steps_of(stream_key, dims, shards, least, high):
    level = 1.0
    for position, parts in shards:
        steps = jax.random.uniform(jax.random.fold_in(jax.random.fold_in(stream_key, 6), position), (parts,), jnp.float32, least / len(shards), high / len(shards))
        level = level * jnp.repeat(jnp.exp(steps), dims[position] // parts).reshape((-1,) + (1,) * (len(dims) - 1 - position))
    return level


def noise(rng, shape, scale, limit, pieces=(), kind=jnp.bfloat16):
    array = jax.random.normal(rng, shape, jnp.float32) * scale
    if len(pieces) > 0:
        array = steps_of(rng, shape, pieces, -0.22, 0.18) * array
    return jnp.clip(array, min=-limit, max=limit).astype(kind)


def setup_inputs(seed: int = 0) -> dict:
    key_of = jax.random.split(jax.random.key(seed), 7)
    box_points = jnp.clip(1.0 * jax.random.uniform(key_of[0], (BOXES, 3, P_SIZE), jnp.float32) ** steps_of(key_of[0], (BOXES, 3, P_SIZE), ((0, 64),), -0.2, 0.2), 0.0, 1.0)
    proxy_directions = draw_proxy_directions(jax.random.fold_in(key_of[6], 71), 0)
    point_order = jax.vmap(lambda own: jax.random.permutation(own, P_SIZE))(jax.random.split(key_of[2], BOXES)).reshape((BOXES, P_SIZE)).astype(jnp.int32)
    neighbour_boxes = draw_neighbour_boxes(jax.random.fold_in(key_of[6], 71), 0)
    neighbour_places = place_ends(jax.random.randint(key_of[4], (BOXES, NB), 0, 26), jax.random.fold_in(key_of[4], 1), 0, 25).astype(jnp.int32)
    pivot_inverse = noise(key_of[5], (BOXES, 2, R), 1.0, 6.0, ((0, 64), (2, 4)), jnp.float32)
    return {"box_points": box_points, "proxy_directions": proxy_directions, "point_order": point_order, "neighbour_boxes": neighbour_boxes, "neighbour_places": neighbour_places, "pivot_inverse": pivot_inverse}


wavenumber = 4.0 * math.pi
softening = 0.05
proxy_radius = 1.5
ridge_share = 0.05
highest = lax.Precision.HIGHEST

def helmholtz(targets, sources):
    distance_sq = jnp.zeros((targets.shape[1], sources.shape[1]), targets.dtype)
    for axis_id in range(3):
        difference = targets[axis_id][:, None] - sources[axis_id][None, :]
        distance_sq = distance_sq + difference * difference
    radius = jnp.sqrt(distance_sq + softening * softening)
    amplitude = 1.0 / (4.0 * math.pi * radius)
    return (amplitude * jnp.cos(wavenumber * radius), amplitude * jnp.sin(wavenumber * radius))

def decode(place_codes):
    full_code = place_codes + (place_codes >= 13).astype(jnp.int32)
    return jnp.stack([full_code // 9 - 1, full_code // 3 % 3 - 1, full_code % 3 - 1], axis=-1).astype(jnp.float32)

def cross_products(real_tile, imag_tile, skel_count):
    stacked = jnp.concatenate([real_tile, imag_tile], axis=0)
    flipped = jnp.concatenate([imag_tile, -real_tile], axis=0)
    left_cols = stacked[:, :skel_count]
    contract = (((0,), (0,)), ((), ()))
    real_cross = lax.dot_general(left_cols.astype(jnp.float32), stacked.astype(jnp.float32), contract, preferred_element_type=jnp.float32)
    imag_cross = lax.dot_general(left_cols.astype(jnp.float32), flipped.astype(jnp.float32), contract, preferred_element_type=jnp.float32)
    return jnp.stack([real_cross, imag_cross])

def factor(gram_block):
    real_gram = gram_block[0]
    imag_gram = gram_block[1]
    skel_count = real_gram.shape[0]
    ridge_value = ridge_share * jnp.trace(real_gram) / skel_count
    real_gram = real_gram + ridge_value * jnp.eye(skel_count, dtype=real_gram.dtype)
    upper_half = jnp.concatenate([real_gram, -imag_gram], axis=1)
    lower_half = jnp.concatenate([imag_gram, real_gram], axis=1)
    return jnp.linalg.cholesky(jnp.concatenate([upper_half, lower_half], axis=0))

def apply_inverse(cholesky_factor, right_side):
    stacked = right_side.reshape(2 * right_side.shape[1], right_side.shape[2])
    forward = lax.linalg.triangular_solve(cholesky_factor, stacked, left_side=True, lower=True)
    backward = lax.linalg.triangular_solve(cholesky_factor, forward, left_side=True, lower=True, transpose_a=True)
    return backward.reshape(right_side.shape)

def pair_update(near_points, own_columns, coefficients, pivot_row):
    skel_count = coefficients.shape[1]
    real_kernel, imag_kernel = helmholtz(near_points, own_columns)
    real_skel = real_kernel[:, :skel_count]
    imag_skel = imag_kernel[:, :skel_count]
    real_rest = real_kernel[:, skel_count:]
    imag_rest = imag_kernel[:, skel_count:]
    matmul_dims = (((1,), (0,)), ((), ()))
    outer_dims = (((1,), (1,)), ((), ()))

    def product(left_side, right_side):
        return lax.dot_general(left_side.astype(jnp.float32), right_side.astype(jnp.float32), matmul_dims, precision=highest, preferred_element_type=jnp.float32)

    def outer_product(left_side, right_side):
        return lax.dot_general(left_side.astype(jnp.float32), right_side.astype(jnp.float32), outer_dims, precision=highest, preferred_element_type=jnp.float32)
    real_block = real_rest - (product(real_skel, coefficients[0]) - product(imag_skel, coefficients[1]))
    imag_block = imag_rest - (product(real_skel, coefficients[1]) + product(imag_skel, coefficients[0]))
    real_weighted = real_block * pivot_row[0][None, :] - imag_block * pivot_row[1][None, :]
    imag_weighted = real_block * pivot_row[1][None, :] + imag_block * pivot_row[0][None, :]
    real_update = outer_product(real_weighted, real_block) - outer_product(imag_weighted, imag_block)
    imag_update = outer_product(real_weighted, imag_block) + outer_product(imag_weighted, real_block)
    return -jnp.stack([real_update, imag_update])

def reference(box_points, proxy_directions, point_order, neighbour_boxes, neighbour_places, pivot_inverse):
    ordered = jnp.take_along_axis(box_points, jnp.broadcast_to(point_order[:, None, :], box_points.shape), axis=2)
    shift_table = decode(neighbour_places)
    proxies = 0.5 + proxy_radius * proxy_directions

    def interp_one(which_box):
        own_points = ordered[which_box]
        near_points = ordered[neighbour_boxes[which_box]] + shift_table[which_box][:, :, None]
        near_points = jnp.transpose(near_points, (1, 0, 2)).reshape(3, NB * P_SIZE)
        targets = jnp.concatenate([proxies, near_points], axis=1)
        real_tile, imag_tile = helmholtz(targets, own_points)
        cross_terms = cross_products(real_tile.astype(jnp.bfloat16), imag_tile.astype(jnp.bfloat16), S)
        cholesky_factor = factor(cross_terms[:, :, :S])
        return apply_inverse(cholesky_factor, cross_terms[:, :, S:])
    interpolation = lax.map(interp_one, jnp.arange(BOXES, dtype=jnp.int32))

    def schur_box(which_box, running):
        own_points = ordered[which_box]
        near_points = ordered[neighbour_boxes[which_box]][:, :, :S] + shift_table[which_box][:, :, None]
        coefficients = interpolation[which_box]
        pivot_row = pivot_inverse[which_box]
        updates = jax.vmap(lambda points_one: pair_update(points_one, own_points, coefficients, pivot_row))(near_points)
        return running.at[neighbour_boxes[which_box]].add(updates)
    skeleton_update = lax.fori_loop(0, BOXES, schur_box, jnp.zeros((BOXES, 2, S, S), jnp.float32))
    return (interpolation, skeleton_update)
```

```python
import math

import jax
import jax.numpy as jnp
import numpy as np
from jax import lax
from jax.experimental import pallas as pl
from jax.experimental.pallas import tpu as pltpu
from jax.sharding import PartitionSpec as P

S = 256
H = 64
NBR = 8
NBOX = 2
f32 = jnp.float32
bf16 = jnp.bfloat16
softening = 0.05
ridge_share = 0.05


def chebyshev_fit(function, count):
    nodes = 0.125 + 0.125 * np.cos(np.pi * (np.arange(256) + 0.5) / 256)
    fit = np.polynomial.chebyshev.Chebyshev.fit(nodes, function(np.sqrt(nodes)), count - 1, domain=[0, 0.25])
    return [float(c) for c in fit.convert(kind=np.polynomial.Polynomial).coef]


SIN_COEF = chebyshev_fit(lambda g: np.sin(np.pi * g) / (g * math.sqrt(math.pi)), 5)
COS_COEF = chebyshev_fit(lambda g: np.cos(np.pi * g) / math.sqrt(math.pi), 5)


def horner(z, coef):
    out = coef[-1]
    for c in coef[-2::-1]:
        out = out * z + c
    return out


def split2(x):
    high = x.astype(bf16)
    return high, (x - high.astype(f32)).astype(bf16)


def split3(x):
    high = x.astype(bf16).astype(f32)
    rest = x - high
    middle = rest.astype(bf16).astype(f32)
    return high, middle, (rest - middle).astype(bf16).astype(f32)


def dot(a, b, rhs_transposed=False, precision=None):
    dims = (((1,), (1 if rhs_transposed else 0,)), ((), ()))
    return lax.dot_general(a, b, dims, precision=precision, preferred_element_type=f32)


def turned(x):
    swapped = pltpu.roll(x, x.shape[1] // 2, 1)
    lane = lax.broadcasted_iota(jnp.int32, x.shape, 1)
    return jnp.where(lane < x.shape[1] // 2, -swapped, swapped)


def expand(x):
    return jnp.concatenate([x, turned(x)], axis=0)


def evaluate(v):
    inv = lax.rsqrt(v)
    turns = v * inv
    g = turns - jnp.round(turns)
    z = g * g
    s = g * horner(z, SIN_COEF)
    c = horner(z, COS_COEF)
    return inv * (1.0 / (2.0 * math.pi) - s * s), inv * (s * c)


def invert(w):
    row_id = lax.broadcasted_iota(jnp.int32, w.shape, 0)
    lane_id = lax.broadcasted_iota(jnp.int32, w.shape, 1)
    line_id = lax.broadcasted_iota(jnp.int32, (1, 2 * H), 1)
    col_id = lax.broadcasted_iota(jnp.int32, (H, 1), 0)
    for k in range(H):
        col_re = w[:, k : k + 1]
        col_im = w[:, H + k : H + k + 1]
        pivot = 1.0 / col_re[k : k + 1]
        row = w[k : k + 1] * pivot
        row = jnp.where(line_id == k, pivot, jnp.where(line_id == H + k, 0.0, row))
        row_turned = turned(row)
        kept = jnp.where((row_id == k) | (lane_id == k) | (lane_id == H + k), 0.0, w)
        col_re = jnp.where(col_id == k, -1.0, col_re)
        col_im = jnp.where(col_id == k, 0.0, col_im)
        w = kept - col_re * row - col_im * row_turned
    return w


def kernel(
    boxes_ref, places_ref, own_ref, before_ref, after_ref, shared_ref,
    interp_ref, update_ref,
    point_ref, source_ref, target_ref, rhs_ref, rest_ref, low_ref, rest_low_ref, z_ref, q_ref,
):
    me = lax.axis_index("box")
    col = lax.axis_index("col")
    total = lax.axis_size("box")
    highest = lax.Precision.HIGHEST

    row8 = lax.broadcasted_iota(jnp.int32, (8, 512), 0)
    for slot in range(6):
        ref = (before_ref, own_ref, after_ref)[slot // 2]
        data = ref[slot % 2]
        order = data[3:4]
        pick = (lax.broadcasted_iota(jnp.int32, (512, 512), 0).astype(f32) == order).astype(bf16)
        parts = split3(2.0 * data - 1.0)
        got = dot(jnp.concatenate(parts + (jnp.zeros_like(data),), axis=0).astype(bf16), pick)
        points = jnp.where(row8[:4] < 3, (got[0:4] + got[4:8]) + got[8:12], 0.0)
        point_ref[slot, 0:4] = points
        point_ref[slot, 4:8] = jnp.zeros_like(points)

    def features(points, is_source):
        width = points.shape[1]
        rows = row8[:, :width]
        square = jnp.sum(points * points, axis=0, keepdims=True)
        if is_source:
            square = square + 4.0 * softening * softening
            scaled = points
        else:
            scaled = -2.0 * points
        high, middle, low = split3(scaled)
        groups = (high, high, middle, high, low, middle) if is_source else (high, middle, high, low, high, middle)
        own_row, other_row = (4, 3) if is_source else (3, 4)
        out = []
        for i, group in enumerate(groups):
            if i < 3:
                part = split3(square)[i]
                group = jnp.where(rows == own_row, part, jnp.where(rows == other_row, 1.0, group))
            out.append(group)
        return jnp.concatenate(out, axis=0)

    for b in range(NBOX):
        source_ref[b] = features(point_ref[2 + b], True).T.astype(bf16)

    slots = []
    back = lax.rem(S - H * col, S)
    for p in range(NBOX * NBR):
        b, k = p // NBR, p % NBR
        box = boxes_ref[b, k]
        code = places_ref[b, k]
        code = code + (code >= 13).astype(jnp.int32)
        step = lax.rem((box >> 1) - me + 1 + total, total)
        slot = step * 2 + (box & 1)
        slots.append(slot)
        dx = (2 * (code // 9) - 2).astype(f32)
        dy = (2 * (code // 3 % 3) - 2).astype(f32)
        dz = (2 * (code % 3) - 2).astype(f32)
        move = jnp.where(row8 == 0, dx, jnp.where(row8 == 1, dy, jnp.where(row8 == 2, dz, 0.0)))
        got = features(point_ref[slot] + move, False)
        target_ref[p] = pltpu.roll(got[:, :S], back, 1).astype(bf16)
        target_ref[16 + p] = got[:, S:].astype(bf16)
    for d in range(4):
        data = shared_ref[d]
        points = jnp.concatenate([jnp.where(row8[:4, :S] < 3, 3.0 * data, 0.0), jnp.zeros_like(data)], axis=0)
        target_ref[32 + d] = features(points, False).astype(bf16)

    flat = jnp.concatenate([shared_ref[d, 3:4] for d in range(4)] + [jnp.zeros((4, S), f32)], axis=0).T
    for b in range(NBOX):
        for part in range(2):
            for d in range(4):
                first = (2 * b + part) * H
                q_ref[b, part, d * H : (d + 1) * H] = jnp.broadcast_to(flat[first : first + H, d : d + 1], (H, 128))

    def tile(b, chunk, keep, place):
        features_t = target_ref[chunk]
        for g in range(8):
            re, im = evaluate(dot(source_ref[b, g * H : (g + 1) * H], features_t))
            re_high, im_high = re.astype(bf16), im.astype(bf16)
            if g < 4:
                top = slice(2 * H * g, 2 * H * g + H)
                bottom = slice(2 * H * g + H, 2 * H * (g + 1))
                rhs_ref[place, top, :S] = re_high
                rhs_ref[place, top, S:] = im_high
                rhs_ref[place, bottom, :S] = -im_high
                rhs_ref[place, bottom, S:] = re_high
            else:
                span = slice(H * (g - 4), H * (g - 3))
                rest_ref[place, span, :S] = re_high
                rest_ref[place, span, S:] = im_high
            if keep:
                re_low = (re - re_high.astype(f32)).astype(bf16)
                im_low = (im - im_high.astype(f32)).astype(bf16)
                if g < 4:
                    low_ref[place, top, :S] = re_low
                    low_ref[place, top, S:] = im_low
                    low_ref[place, bottom, :S] = -im_low
                    low_ref[place, bottom, S:] = re_low
                else:
                    rest_low_ref[place, span, :S] = re_low
                    rest_low_ref[place, span, S:] = im_low
        left = jnp.concatenate(
            [rhs_ref[place, 2 * H * g : 2 * H * g + H] for g in range(4)] + [rest_ref[place]], axis=0
        )
        got = dot(left, rhs_ref[place], rhs_transposed=True)
        for c in range(4):
            z_ref[b, c] += got[:, 2 * H * c : 2 * H * (c + 1)]

    z_ref[...] = jnp.zeros_like(z_ref)
    for b in range(NBOX):

        @pl.loop(0, NBR)
        def _(k):
            tile(b, b * NBR + k, True, b * NBR + k)

        @pl.loop(0, NBR + 4)
        def _(k):
            tile(b, jnp.where(k < NBR, 16 + b * NBR + k, 24 + k), False, 16)

    for b in range(NBOX):
        row_id = lax.broadcasted_iota(jnp.int32, (H, 2 * H), 0)
        lane_id = lax.broadcasted_iota(jnp.int32, (H, 2 * H), 1)
        on_diagonal = row_id == lane_id
        trace = jnp.zeros((1, 1), f32)
        for c in range(4):
            block = jnp.where(on_diagonal, z_ref[b, c, c * H : (c + 1) * H], 0.0)
            trace = trace + jnp.sum(jnp.sum(block, axis=0, keepdims=True), axis=1, keepdims=True)
        ridge = jnp.where(on_diagonal, ridge_share * trace / S, 0.0)
        for c in range(4):
            z_ref[b, c, c * H : (c + 1) * H] += ridge

    @pl.loop(0, 4)
    def _(kb):
        rows = pl.ds(pl.multiple_of(kb * H, H), H)
        inverses = [invert(z_ref[b, kb, rows]) for b in range(NBOX)]
        for b in range(NBOX):
            block = dot(z_ref[b, kb], expand(inverses[b]), precision=highest)
            z_ref[b, kb] = block
            for t in range(1, 4):
                c = lax.rem(kb + t, 4)
                z_ref[b, c] -= dot(block, expand(z_ref[b, c, rows]), precision=highest)

    mine = pl.ds(pl.multiple_of(col * H, H), H)
    for b in range(NBOX):
        for c in range(4):
            across = z_ref[b, c, pl.ds(pl.multiple_of(S + col * H, H), H)].T
            interp_ref[b, 0, c * H : (c + 1) * H] = across[:H]
            interp_ref[b, 1, c * H : (c + 1) * H] = across[H:]

    update_ref[...] = jnp.zeros_like(update_ref)
    for b in range(NBOX):
        x = jnp.concatenate([z_ref[b, c, S:] for c in range(4)], axis=1)
        x_high, x_low = split2(x)
        x_both = jnp.concatenate([x_high, x_low], axis=0)
        for k in range(NBR):
            p = b * NBR + k
            both = dot(x_both, rhs_ref[p])
            block = (rest_ref[p].astype(f32) + rest_low_ref[p].astype(f32)) - (
                (both[:S] + both[S:]) + dot(x_high, low_ref[p])
            )
            first = jnp.concatenate([block[:, :H], block[:, S : S + H]], axis=1)
            weighted = (q_ref[b, 0] * first + q_ref[b, 1] * turned(first)).T
            left = jnp.concatenate([weighted, jnp.concatenate([-weighted[H:], weighted[:H]], axis=0)], axis=1)
            left_high, left_low = split2(left)
            right = jnp.concatenate([block[:, :S], block[:, S:]], axis=0)
            right_high, right_low = split2(right)
            got = dot(jnp.concatenate([left_high, left_low], axis=0), right_high)
            update_ref[slots[p]] -= (got[: 2 * H] + got[2 * H :]) + dot(left_high, right_low)
    for slot in range(6):
        update_ref[slot] = pltpu.roll(update_ref[slot], H * col, 1)


def on_device(
    box_points, proxy_directions, point_order, neighbour_boxes, neighbour_places, pivot_inverse
):
    count = lax.axis_size("box")
    forward = [(i, (i + 1) % count) for i in range(count)]
    backward = [((i + 1) % count, i) for i in range(count)]
    own = jnp.concatenate([box_points, point_order.astype(f32)[:, None, :]], axis=1)
    before = lax.ppermute(own, "box", forward)
    after = lax.ppermute(own, "box", backward)
    shared = lax.all_gather(
        jnp.concatenate([proxy_directions, pivot_inverse.reshape(1, S)], axis=0), "col"
    )
    smem = pl.BlockSpec(memory_space=pltpu.SMEM)
    vmem = pl.BlockSpec(memory_space=pltpu.VMEM)
    interpolation, update = pl.pallas_call(
        kernel,
        out_shape=(
            jax.ShapeDtypeStruct((NBOX, 2, S, H), f32),
            jax.ShapeDtypeStruct((6, 2 * H, S), f32),
        ),
        in_specs=[smem, smem, vmem, vmem, vmem, vmem],
        out_specs=(vmem, vmem),
        scratch_shapes=[
            pltpu.VMEM((6, 8, 512), f32),
            pltpu.VMEM((NBOX, 512, 48), bf16),
            pltpu.VMEM((36, 48, S), bf16),
            pltpu.VMEM((17, 512, 512), bf16),
            pltpu.VMEM((17, S, 512), bf16),
            pltpu.VMEM((16, 512, 512), bf16),
            pltpu.VMEM((16, S, 512), bf16),
            pltpu.VMEM((NBOX, 4, 512, 2 * H), f32),
            pltpu.VMEM((NBOX, 2, S, 128), f32),
        ],
        compiler_params=pltpu.CompilerParams(vmem_limit_bytes=60 * 1024 * 1024),
        name="skeletonize",
    )(neighbour_boxes, neighbour_places, own, before, after, shared)
    update = update.reshape(6, 2, H, S)
    from_before = lax.ppermute(update[4:6], "box", forward)
    from_after = lax.ppermute(update[0:2], "box", backward)
    return (interpolation, update[2:4] + from_before + from_after)


def solution(mesh):
    placed = (
        P("box", None, None),
        P(None, "col"),
        P("box", None),
        P("box", None),
        P("box", None),
        P("box", None, "col"),
    )
    return jax.shard_map(
        on_device,
        mesh=mesh,
        in_specs=placed,
        out_specs=(P("box", None, None, "col"), P("box", None, "col", None)),
        check_vma=False,
    )
```

```python
import math

import jax
import jax.numpy as jnp
import numpy as np
from jax import lax
from jax.experimental import pallas as pl
from jax.experimental.pallas import tpu as pltpu
from jax.sharding import PartitionSpec as P

S = 256
H = 64
NBR = 8
NBOX = 2
f32 = jnp.float32
bf16 = jnp.bfloat16
softening = 0.05
ridge_share = 0.05


def chebyshev_fit(function, count):
    nodes = 0.125 + 0.125 * np.cos(np.pi * (np.arange(256) + 0.5) / 256)
    fit = np.polynomial.chebyshev.Chebyshev.fit(nodes, function(np.sqrt(nodes)), count - 1, domain=[0, 0.25])
    return [float(c) for c in fit.convert(kind=np.polynomial.Polynomial).coef]


SIN_COEF = chebyshev_fit(lambda g: np.sin(np.pi * g) / (g * math.sqrt(math.pi)), 5)
COS_COEF = chebyshev_fit(lambda g: np.cos(np.pi * g) / math.sqrt(math.pi), 5)


def horner(z, coef):
    out = coef[-1]
    for c in coef[-2::-1]:
        out = out * z + c
    return out


def split2(x):
    high = x.astype(bf16)
    return high, (x - high.astype(f32)).astype(bf16)


def split3(x):
    high = x.astype(bf16).astype(f32)
    rest = x - high
    middle = rest.astype(bf16).astype(f32)
    return high, middle, (rest - middle).astype(bf16).astype(f32)


def dot(a, b, rhs_transposed=False, precision=None):
    dims = (((1,), (1 if rhs_transposed else 0,)), ((), ()))
    return lax.dot_general(a, b, dims, precision=precision, preferred_element_type=f32)


def turned(x):
    swapped = pltpu.roll(x, x.shape[1] // 2, 1)
    lane = lax.broadcasted_iota(jnp.int32, x.shape, 1)
    return jnp.where(lane < x.shape[1] // 2, -swapped, swapped)


def expand(x):
    return jnp.concatenate([x, turned(x)], axis=0)


def evaluate(v):
    inv = lax.rsqrt(v)
    turns = v * inv
    g = turns - jnp.round(turns)
    z = g * g
    s = g * horner(z, SIN_COEF)
    c = horner(z, COS_COEF)
    return inv * (1.0 / (2.0 * math.pi) - s * s), inv * (s * c)


def times(a, b):
    return a[0] * b[0] - a[1] * b[1], a[0] * b[1] + a[1] * b[0]


def invert(w):
    shape = (8, 2 * H)
    row_id = lax.broadcasted_iota(jnp.int32, shape, 0)
    lane_id = lax.broadcasted_iota(jnp.int32, shape, 1)
    line_id = lax.broadcasted_iota(jnp.int32, (1, 2 * H), 1)
    groups = [w[8 * g : 8 * g + 8] for g in range(H // 8)]
    for p in range(H // 8):
        columns = [
            [
                tuple(jnp.broadcast_to(w_g[:, at : at + 1], shape) for at in (8 * p + j, H + 8 * p + j))
                for j in range(8)
            ]
            for w_g in groups
        ]
        rows = groups[p]
        rows_t = turned(rows)
        small = list(columns[p])
        for j in range(8):
            at = 8 * p + j
            pivot = 1.0 / small[j][0][j : j + 1]
            row = jnp.where(line_id == at, pivot, jnp.where(line_id == H + at, 0.0, rows[j : j + 1] * pivot))
            row_t = jnp.where(line_id == H + at, pivot, jnp.where(line_id == at, 0.0, rows_t[j : j + 1] * pivot))
            here = row_id == j
            re = jnp.where(here, -1.0, small[j][0])
            im = jnp.where(here, 0.0, small[j][1])
            out = here | (lane_id == at) | (lane_id == H + at)
            rows = jnp.where(out, 0.0, rows) - re * row - im * row_t
            rows_t = jnp.where(out, 0.0, rows_t) - re * row_t + im * row
            for l in range(j + 1, 8):
                factor = tuple(x[j : j + 1] * pivot for x in small[l])
                step = times((re, im), factor)
                small[l] = tuple(jnp.where(here, 0.0, x) - y for x, y in zip(small[l], step))
        panel = ((lane_id >= 8 * p) & (lane_id < 8 * p + 8)) | ((lane_id >= H + 8 * p) & (lane_id < H + 8 * p + 8))
        for g in range(H // 8):
            if g == p:
                groups[g] = rows
                continue
            terms = [
                columns[g][j][0] * rows[j : j + 1] + columns[g][j][1] * rows_t[j : j + 1] for j in range(8)
            ]
            while len(terms) > 1:
                terms = [x + y for x, y in zip(terms[::2], terms[1::2])]
            groups[g] = jnp.where(panel, 0.0, groups[g]) - terms[0]
    return jnp.concatenate(groups, axis=0)


def kernel(
    boxes_ref, places_ref, own_ref, before_ref, after_ref, shared_ref,
    interp_ref, update_ref,
    point_ref, source_ref, target_ref, rhs_ref, rest_ref, low_ref, rest_low_ref, z_ref, q_ref,
    main0_ref, side0_ref, main1_ref, side1_ref,
):
    me = lax.axis_index("box")
    col = lax.axis_index("col")
    total = lax.axis_size("box")
    highest = lax.Precision.HIGHEST

    row8 = lax.broadcasted_iota(jnp.int32, (8, 512), 0)
    for slot in range(6):
        ref = (before_ref, own_ref, after_ref)[slot // 2]
        data = ref[slot % 2]
        order = data[3:4]
        pick = (lax.broadcasted_iota(jnp.int32, (512, 512), 0).astype(f32) == order).astype(bf16)
        parts = split3(2.0 * data - 1.0)
        got = dot(jnp.concatenate(parts + (jnp.zeros_like(data),), axis=0).astype(bf16), pick)
        points = jnp.where(row8[:4] < 3, (got[0:4] + got[4:8]) + got[8:12], 0.0)
        point_ref[slot, 0:4] = points
        point_ref[slot, 4:8] = jnp.zeros_like(points)

    def features(points, is_source):
        width = points.shape[1]
        rows = row8[:, :width]
        square = jnp.sum(points * points, axis=0, keepdims=True)
        if is_source:
            square = square + 4.0 * softening * softening
            scaled = points
        else:
            scaled = -2.0 * points
        high, middle, low = split3(scaled)
        groups = (high, high, middle, high, low, middle) if is_source else (high, middle, high, low, high, middle)
        own_row, other_row = (4, 3) if is_source else (3, 4)
        out = []
        for i, group in enumerate(groups):
            if i < 3:
                part = split3(square)[i]
                group = jnp.where(rows == own_row, part, jnp.where(rows == other_row, 1.0, group))
            out.append(group)
        return jnp.concatenate(out, axis=0)

    for b in range(NBOX):
        source_ref[b] = features(point_ref[2 + b], True).T.astype(bf16)

    slots = []
    back = lax.rem(S - H * col, S)
    for p in range(NBOX * NBR):
        b, k = p // NBR, p % NBR
        box = boxes_ref[b, k]
        code = places_ref[b, k]
        code = code + (code >= 13).astype(jnp.int32)
        step = lax.rem((box >> 1) - me + 1 + total, total)
        slot = step * 2 + (box & 1)
        slots.append(slot)
        dx = (2 * (code // 9) - 2).astype(f32)
        dy = (2 * (code // 3 % 3) - 2).astype(f32)
        dz = (2 * (code % 3) - 2).astype(f32)
        move = jnp.where(row8 == 0, dx, jnp.where(row8 == 1, dy, jnp.where(row8 == 2, dz, 0.0)))
        got = features(point_ref[slot] + move, False)
        target_ref[p] = pltpu.roll(got[:, :S], back, 1).astype(bf16)
        target_ref[16 + p] = got[:, S:].astype(bf16)
    for d in range(4):
        data = shared_ref[d]
        points = jnp.concatenate([jnp.where(row8[:4, :S] < 3, 3.0 * data, 0.0), jnp.zeros_like(data)], axis=0)
        target_ref[32 + d] = features(points, False).astype(bf16)

    flat = jnp.concatenate([shared_ref[d, 3:4] for d in range(4)] + [jnp.zeros((4, S), f32)], axis=0).T
    for b in range(NBOX):
        for part in range(2):
            for d in range(4):
                first = (2 * b + part) * H
                q_ref[b, part, d * H : (d + 1) * H] = jnp.broadcast_to(flat[first : first + H, d : d + 1], (H, 128))

    def tile(b, chunk, out_refs, p):
        main_ref, side_ref = out_refs
        features_t = target_ref[chunk]
        for g in range(8):
            re, im = evaluate(dot(source_ref[b, g * H : (g + 1) * H], features_t))
            re_high, im_high = re.astype(bf16), im.astype(bf16)
            high = jnp.concatenate([re_high, im_high], axis=1)
            if g < 4:
                span = slice(2 * H * g, 2 * H * (g + 1))
                high = jnp.concatenate([high, jnp.concatenate([-im_high, re_high], axis=1)], axis=0)
                main_ref[span] = high
            else:
                span = slice(H * (g - 4), H * (g - 3))
                side_ref[span] = high
            if p is None:
                continue
            re_low = (re - re_high.astype(f32)).astype(bf16)
            im_low = (im - im_high.astype(f32)).astype(bf16)
            low = jnp.concatenate([re_low, im_low], axis=1)
            if g < 4:
                low = jnp.concatenate([low, jnp.concatenate([-im_low, re_low], axis=1)], axis=0)
                rhs_ref[p, span] = high
                low_ref[p, span] = low
            else:
                rest_ref[p, span] = high
                rest_low_ref[p, span] = low

    def gram(b, in_refs):
        main_ref, side_ref = in_refs
        left = jnp.concatenate(
            [main_ref[2 * H * g : 2 * H * g + H] for g in range(4)] + [side_ref[...]], axis=0
        )
        got = dot(left, main_ref[...], rhs_transposed=True)
        for c in range(4):
            z_ref[b, c] += got[:, 2 * H * c : 2 * H * (c + 1)]

    z_ref[...] = jnp.zeros_like(z_ref)
    even, odd = (main0_ref, side0_ref), (main1_ref, side1_ref)
    main1_ref[...] = jnp.zeros_like(main1_ref)
    side1_ref[...] = jnp.zeros_like(side1_ref)
    for b in range(NBOX):
        first = b * NBR

        @pl.loop(0, NBR // 2)
        def _(k):
            gram(b, odd)
            tile(b, first + 2 * k, even, first + 2 * k)
            gram(b, even)
            tile(b, first + 2 * k + 1, odd, first + 2 * k + 1)

        @pl.loop(0, NBR // 2 + 2)
        def _(k):
            chunk = jnp.where(k < NBR // 2, 16 + first + 2 * k, 24 + 2 * k)
            gram(b, odd)
            tile(b, chunk, even, None)
            gram(b, even)
            tile(b, chunk + 1, odd, None)

        gram(b, odd)
        if b + 1 < NBOX:
            main1_ref[...] = jnp.zeros_like(main1_ref)
            side1_ref[...] = jnp.zeros_like(side1_ref)

    for b in range(NBOX):
        row_id = lax.broadcasted_iota(jnp.int32, (H, 2 * H), 0)
        lane_id = lax.broadcasted_iota(jnp.int32, (H, 2 * H), 1)
        on_diagonal = row_id == lane_id
        trace = jnp.zeros((1, 1), f32)
        for c in range(4):
            block = jnp.where(on_diagonal, z_ref[b, c, c * H : (c + 1) * H], 0.0)
            trace = trace + jnp.sum(jnp.sum(block, axis=0, keepdims=True), axis=1, keepdims=True)
        ridge = jnp.where(on_diagonal, ridge_share * trace / S, 0.0)
        for c in range(4):
            z_ref[b, c, c * H : (c + 1) * H] += ridge

    inverses = [invert(z_ref[b, 0, :H]) for b in range(NBOX)]
    for kb in range(4):
        rows = slice(kb * H, (kb + 1) * H)
        below = slice((kb + 1) * H, 512)
        following = slice((kb + 1) * H, (kb + 2) * H)
        spread = [expand(x) for x in inverses]
        blocks, others = [], []
        for b in range(NBOX):
            blocks.append(z_ref[b, kb, below])
            others.append({c: expand(z_ref[b, c, rows]) for c in range(4) if c != kb})
        if kb < 3:
            inverses = []
            for b in range(NBOX):
                top = dot(blocks[b][:H], spread[b], precision=highest)
                inverses.append(
                    invert(z_ref[b, kb + 1, following] - dot(top, others[b][kb + 1], precision=highest))
                )
        for b in range(NBOX):
            block = dot(blocks[b], spread[b], precision=highest)
            z_ref[b, kb, below] = block
            step = dot(block, jnp.concatenate(list(others[b].values()), axis=1), precision=highest)
            for i, c in enumerate(others[b]):
                z_ref[b, c, below] -= step[:, 2 * H * i : 2 * H * (i + 1)]

    for b in range(NBOX):
        for c in range(4):
            across = z_ref[b, c, pl.ds(pl.multiple_of(S + col * H, H), H)].T
            interp_ref[b, 0, c * H : (c + 1) * H] = across[:H]
            interp_ref[b, 1, c * H : (c + 1) * H] = across[H:]

    update_ref[...] = jnp.zeros_like(update_ref)
    for b in range(NBOX):
        x = jnp.concatenate([z_ref[b, c, S:] for c in range(4)], axis=1)
        x_high, x_low = split2(x)
        x_both = jnp.concatenate([x_high, x_low], axis=0)
        for k in range(NBR):
            p = b * NBR + k
            both = dot(x_both, rhs_ref[p])
            block = (rest_ref[p].astype(f32) + rest_low_ref[p].astype(f32)) - (
                (both[:S] + both[S:]) + dot(x_high, low_ref[p])
            )
            first = jnp.concatenate([block[:, :H], block[:, S : S + H]], axis=1)
            weighted = (q_ref[b, 0] * first + q_ref[b, 1] * turned(first)).T
            left = jnp.concatenate([weighted, jnp.concatenate([-weighted[H:], weighted[:H]], axis=0)], axis=1)
            left_high, left_low = split2(left)
            right = jnp.concatenate([block[:, :S], block[:, S:]], axis=0)
            right_high, right_low = split2(right)
            got = dot(jnp.concatenate([left_high, left_low], axis=0), right_high)
            update_ref[slots[p]] -= (got[: 2 * H] + got[2 * H :]) + dot(left_high, right_low)
    for slot in range(6):
        update_ref[slot] = pltpu.roll(update_ref[slot], H * col, 1)


def on_device(
    box_points, proxy_directions, point_order, neighbour_boxes, neighbour_places, pivot_inverse
):
    count = lax.axis_size("box")
    forward = [(i, (i + 1) % count) for i in range(count)]
    backward = [((i + 1) % count, i) for i in range(count)]
    own = jnp.concatenate([box_points, point_order.astype(f32)[:, None, :]], axis=1)
    before = lax.ppermute(own, "box", forward)
    after = lax.ppermute(own, "box", backward)
    shared = lax.all_gather(
        jnp.concatenate([proxy_directions, pivot_inverse.reshape(1, S)], axis=0), "col"
    )
    smem = pl.BlockSpec(memory_space=pltpu.SMEM)
    vmem = pl.BlockSpec(memory_space=pltpu.VMEM)
    interpolation, update = pl.pallas_call(
        kernel,
        out_shape=(
            jax.ShapeDtypeStruct((NBOX, 2, S, H), f32),
            jax.ShapeDtypeStruct((6, 2 * H, S), f32),
        ),
        in_specs=[smem, smem, vmem, vmem, vmem, vmem],
        out_specs=(vmem, vmem),
        scratch_shapes=[
            pltpu.VMEM((6, 8, 512), f32),
            pltpu.VMEM((NBOX, 512, 48), bf16),
            pltpu.VMEM((36, 48, S), bf16),
            pltpu.VMEM((16, 512, 512), bf16),
            pltpu.VMEM((16, S, 512), bf16),
            pltpu.VMEM((16, 512, 512), bf16),
            pltpu.VMEM((16, S, 512), bf16),
            pltpu.VMEM((NBOX, 4, 512, 2 * H), f32),
            pltpu.VMEM((NBOX, 2, S, 128), f32),
            pltpu.VMEM((512, 512), bf16),
            pltpu.VMEM((S, 512), bf16),
            pltpu.VMEM((512, 512), bf16),
            pltpu.VMEM((S, 512), bf16),
        ],
        compiler_params=pltpu.CompilerParams(vmem_limit_bytes=60 * 1024 * 1024),
        name="skeletonize",
    )(neighbour_boxes, neighbour_places, own, before, after, shared)
    update = update.reshape(6, 2, H, S)
    from_before = lax.ppermute(update[4:6], "box", forward)
    from_after = lax.ppermute(update[0:2], "box", backward)
    return (interpolation, update[2:4] + from_before + from_after)


def solution(mesh):
    placed = (
        P("box", None, None),
        P(None, "col"),
        P("box", None),
        P("box", None),
        P("box", None),
        P("box", None, "col"),
    )
    return jax.shard_map(
        on_device,
        mesh=mesh,
        in_specs=placed,
        out_specs=(P("box", None, None, "col"), P("box", None, "col", None)),
        check_vma=False,
    )
```

```python
import math

import jax
import jax.numpy as jnp
import numpy as np
from jax import lax
from jax.experimental import pallas as pl
from jax.experimental.pallas import tpu as pltpu
from jax.sharding import PartitionSpec as P

S = 256
H = 64
NBR = 8
NBOX = 2
f32 = jnp.float32
bf16 = jnp.bfloat16
softening = 0.05
ridge_share = 0.05


def chebyshev_fit(function, count):
    nodes = 0.125 + 0.125 * np.cos(np.pi * (np.arange(256) + 0.5) / 256)
    fit = np.polynomial.chebyshev.Chebyshev.fit(nodes, function(np.sqrt(nodes)), count - 1, domain=[0, 0.25])
    return [float(c) for c in fit.convert(kind=np.polynomial.Polynomial).coef]


SIN_COEF = chebyshev_fit(lambda g: np.sin(np.pi * g) / (g * math.sqrt(math.pi)), 5)
COS_COEF = chebyshev_fit(lambda g: np.cos(np.pi * g) / math.sqrt(math.pi), 5)


def horner(z, coef):
    out = coef[-1]
    for c in coef[-2::-1]:
        out = out * z + c
    return out


def split2(x):
    high = x.astype(bf16)
    return high, (x - high.astype(f32)).astype(bf16)


def split3(x):
    high = x.astype(bf16).astype(f32)
    rest = x - high
    middle = rest.astype(bf16).astype(f32)
    return high, middle, (rest - middle).astype(bf16).astype(f32)


def dot(a, b, rhs_transposed=False, precision=None):
    dims = (((1,), (1 if rhs_transposed else 0,)), ((), ()))
    return lax.dot_general(a, b, dims, precision=precision, preferred_element_type=f32)


def turned(x):
    swapped = pltpu.roll(x, x.shape[1] // 2, 1)
    lane = lax.broadcasted_iota(jnp.int32, x.shape, 1)
    return jnp.where(lane < x.shape[1] // 2, -swapped, swapped)


def expand(x):
    return jnp.concatenate([x, turned(x)], axis=0)


def evaluate(v):
    inv = lax.rsqrt(v)
    turns = v * inv
    g = turns - jnp.round(turns)
    z = g * g
    s = g * horner(z, SIN_COEF)
    c = horner(z, COS_COEF)
    return inv * (1.0 / (2.0 * math.pi) - s * s), inv * (s * c)


def times(a, b):
    return a[0] * b[0] - a[1] * b[1], a[0] * b[1] + a[1] * b[0]


def invert(w):
    shape = (8, 2 * H)
    row_id = lax.broadcasted_iota(jnp.int32, shape, 0)
    lane_id = lax.broadcasted_iota(jnp.int32, shape, 1)
    line_id = lax.broadcasted_iota(jnp.int32, (1, 2 * H), 1)
    groups = [w[8 * g : 8 * g + 8] for g in range(H // 8)]
    for p in range(H // 8):
        columns = [
            [
                tuple(jnp.broadcast_to(w_g[:, at : at + 1], shape) for at in (8 * p + j, H + 8 * p + j))
                for j in range(8)
            ]
            for w_g in groups
        ]
        rows = groups[p]
        rows_t = turned(rows)
        small = list(columns[p])
        for j in range(8):
            at = 8 * p + j
            pivot = 1.0 / small[j][0][j : j + 1]
            row = jnp.where(line_id == at, pivot, jnp.where(line_id == H + at, 0.0, rows[j : j + 1] * pivot))
            row_t = jnp.where(line_id == H + at, pivot, jnp.where(line_id == at, 0.0, rows_t[j : j + 1] * pivot))
            here = row_id == j
            re = jnp.where(here, -1.0, small[j][0])
            im = jnp.where(here, 0.0, small[j][1])
            out = here | (lane_id == at) | (lane_id == H + at)
            rows = jnp.where(out, 0.0, rows) - re * row - im * row_t
            rows_t = jnp.where(out, 0.0, rows_t) - re * row_t + im * row
            for l in range(j + 1, 8):
                factor = tuple(x[j : j + 1] * pivot for x in small[l])
                step = times((re, im), factor)
                small[l] = tuple(jnp.where(here, 0.0, x) - y for x, y in zip(small[l], step))
        panel = ((lane_id >= 8 * p) & (lane_id < 8 * p + 8)) | ((lane_id >= H + 8 * p) & (lane_id < H + 8 * p + 8))
        for g in range(H // 8):
            if g == p:
                groups[g] = rows
                continue
            terms = [
                columns[g][j][0] * rows[j : j + 1] + columns[g][j][1] * rows_t[j : j + 1] for j in range(8)
            ]
            while len(terms) > 1:
                terms = [x + y for x, y in zip(terms[::2], terms[1::2])]
            groups[g] = jnp.where(panel, 0.0, groups[g]) - terms[0]
    return jnp.concatenate(groups, axis=0)


def on_diagonals(shape):
    return lax.broadcasted_iota(jnp.int32, shape, 0) == lax.broadcasted_iota(jnp.int32, shape, 1)


def row_ids(width):
    return lax.broadcasted_iota(jnp.int32, (8, width), 0)


def ordered(data):
    pick = (lax.broadcasted_iota(jnp.int32, (512, 512), 0).astype(f32) == data[3:4]).astype(bf16)
    parts = split3(2.0 * data - 1.0)
    got = dot(jnp.concatenate(parts + (jnp.zeros_like(data),), axis=0).astype(bf16), pick)
    points = jnp.where(row_ids(512)[:4] < 3, (got[0:4] + got[4:8]) + got[8:12], 0.0)
    return jnp.concatenate([points, jnp.zeros_like(points)], axis=0)


def features(points, is_source):
    rows = row_ids(points.shape[1])
    square = jnp.sum(points * points, axis=0, keepdims=True)
    if is_source:
        square = square + 4.0 * softening * softening
        high, middle, low = split3(points)
        groups = (high, high, middle, high, low, middle)
    else:
        high, middle, low = split3(-2.0 * points)
        groups = (high, middle, high, low, high, middle)
    own_row, other_row = (4, 3) if is_source else (3, 4)
    squares = split3(square)
    out = [
        jnp.where(rows == own_row, squares[i], jnp.where(rows == other_row, 1.0, group)) if i < 3 else group
        for i, group in enumerate(groups)
    ]
    return jnp.concatenate(out, axis=0)


def pair_step(boxes_ref, b, k):
    me, total = lax.axis_index("box"), lax.axis_size("box")
    box = boxes_ref[b, k]
    return lax.rem((box >> 1) - me + 1 + total, total), box & 1


def list_pairs(boxes_ref, list_ref, own):
    found = jnp.int32(0)
    for p in range(NBOX * NBR):
        step, _ = pair_step(boxes_ref, p // NBR, p % NBR)
        fits = (step == 1) if own else (step != 1)

        @pl.when(fits & (found < NBR))
        def _():
            list_ref[found] = p

        found = found + fits.astype(jnp.int32)


def pair_features(places_ref, points, b, k):
    code = places_ref[b, k]
    code = code + (code >= 13).astype(jnp.int32)
    rows = row_ids(512)
    move = jnp.zeros((8, 512), f32)
    for axis, digit in enumerate((code // 9, code // 3 % 3, code % 3)):
        move = jnp.where(rows == axis, (2 * digit - 2).astype(f32), move)
    got = features(points + move, False)
    back = lax.rem(S - H * lax.axis_index("col"), S)
    return pltpu.roll(got[:, :S], back, 1).astype(bf16), got[:, S:].astype(bf16)


def gram_piece(z_ref, b, in_refs, piece):
    main_ref, side_ref = in_refs
    half, n0 = piece
    if half == 0:
        left = jnp.concatenate([main_ref[2 * H * g : 2 * H * g + H] for g in range(4)], axis=0)
    else:
        left = side_ref[...]
    got = dot(left, main_ref[n0 : n0 + S], rhs_transposed=True)
    for i in range(2):
        z_ref[b, n0 // 128 + i, S * half : S * (half + 1)] += got[:, 2 * H * i : 2 * H * (i + 1)]


PIECES = {0: (0, 0), 2: (1, 0), 4: (0, S), 6: (1, S)}


def tile(source_ref, b, features_t, out_refs, kept, z_ref, b_in, in_refs):
    main_ref, side_ref = out_refs
    for g in range(8):
        if g in PIECES:
            gram_piece(z_ref, b_in, in_refs, PIECES[g])
        re, im = evaluate(dot(source_ref[b, g * H : (g + 1) * H], features_t))
        re_high, im_high = re.astype(bf16), im.astype(bf16)
        high = jnp.concatenate([re_high, im_high], axis=1)
        if g < 4:
            span = slice(2 * H * g, 2 * H * (g + 1))
            high = jnp.concatenate([high, jnp.concatenate([-im_high, re_high], axis=1)], axis=0)
            main_ref[span] = high
        else:
            span = slice(H * (g - 4), H * (g - 3))
            side_ref[span] = high
        if kept is None:
            continue
        i, rhs_ref, low_ref, rest_ref, rest_low_ref = kept
        re_low = (re - re_high.astype(f32)).astype(bf16)
        im_low = (im - im_high.astype(f32)).astype(bf16)
        low = jnp.concatenate([re_low, im_low], axis=1)
        if g < 4:
            low = jnp.concatenate([low, jnp.concatenate([-im_low, re_low], axis=1)], axis=0)
            rhs_ref[i, span] = high
            low_ref[i, span] = low
        else:
            rest_ref[i, span] = high
            rest_low_ref[i, span] = low


def pair_tiles(boxes_ref, places_ref, list_ref, source_ref, points_of, kept, z_ref, even, odd, after_each=None):
    for ref in odd:
        ref[...] = jnp.zeros_like(ref)

    @pl.loop(0, NBR)
    def _(i):
        p = list_ref[i]
        b_last = list_ref[jnp.maximum(i - 1, 0)] >> 3
        b, k = p >> 3, p & 7
        skeleton, redundant = pair_features(places_ref, points_of(b, k), b, k)
        tile(source_ref, b, skeleton, even, (i,) + kept, z_ref, b_last, odd)
        if after_each is not None:
            after_each(i)
        tile(source_ref, b, redundant, odd, None, z_ref, b, even)


def put_pivots(q_ref, shared):
    col = lax.axis_index("col")
    flat = jnp.concatenate([ref[3:4] for ref in shared] + [jnp.zeros((4, S), f32)], axis=0).T
    for b in range(NBOX):
        for part in range(2):
            first = (2 * b + part) * H
            for shift in range(4):
                rows = pl.ds(pl.multiple_of(lax.rem(col - shift + 4, 4) * H, H), H)
                q_ref[b, part, rows] = jnp.broadcast_to(flat[first : first + H, shift : shift + 1], (H, 128))


def pair_update(x_ref, q_ref, b, rhs, low, rest):
    x_both = x_ref[b]
    both = dot(x_both, rhs)
    block = rest - ((both[:S] + both[S:]) + dot(x_both[:S], low))
    first = jnp.concatenate([block[:, :H], block[:, S : S + H]], axis=1)
    weighted = (q_ref[b, 0] * first + q_ref[b, 1] * turned(first)).T
    left = jnp.concatenate([weighted, jnp.concatenate([-weighted[H:], weighted[:H]], axis=0)], axis=1)
    left_high, left_low = split2(left)
    right_high, right_low = split2(jnp.concatenate([block[:, :S], block[:, S:]], axis=0))
    got = dot(jnp.concatenate([left_high, left_low], axis=0), right_high)
    return (got[: 2 * H] + got[2 * H :]) + dot(left_high, right_low)


def put_x(x_ref, x, b):
    high, low = split2(x)
    x_ref[b, :S] = high
    x_ref[b, S:] = low


def own_tiles(
    boxes_ref, places_ref, own_ref,
    z_ref, source_ref, rhs_out, low_out, rest_out, rest_low_out,
    list_ref, point_ref, rhs_ref, low_ref, rest_ref, rest_low_ref, main0_ref, side0_ref, main1_ref, side1_ref, sems,
):
    list_pairs(boxes_ref, list_ref, True)
    for b in range(NBOX):
        point_ref[b] = ordered(own_ref[b])
        source_ref[b] = features(point_ref[b], True).T.astype(bf16)
    z_ref[...] = jnp.zeros_like(z_ref)
    even, odd = (main0_ref, side0_ref), (main1_ref, side1_ref)
    kept = (rhs_ref, low_ref, rest_ref, rest_low_ref)
    outs = (rhs_out, low_out, rest_out, rest_low_out)

    def copies(i):
        return [pltpu.make_async_copy(src.at[i], dst.at[i], sems.at[i, n]) for n, (src, dst) in enumerate(zip(kept, outs))]

    def start(i):
        for copy in copies(i):
            copy.start()

    pair_tiles(
        boxes_ref, places_ref, list_ref, source_ref,
        lambda b, k: point_ref[pair_step(boxes_ref, b, k)[1]],
        kept, z_ref, even, odd, start,
    )
    for piece in PIECES.values():
        gram_piece(z_ref, list_ref[NBR - 1] >> 3, odd, piece)
    for i in range(NBR):
        for copy in copies(i):
            copy.wait()


def solve(z_ref):
    highest = lax.Precision.HIGHEST
    on_diagonal = on_diagonals((H, 2 * H))
    for b in range(NBOX):
        total = jnp.zeros((H, 2 * H), f32)
        for c in range(4):
            total = total + jnp.where(on_diagonal, z_ref[b, c, c * H : (c + 1) * H], 0.0)
        trace = jnp.sum(jnp.sum(total, axis=0, keepdims=True), axis=1, keepdims=True)
        ridge = jnp.where(on_diagonal, ridge_share * trace / S, 0.0)
        for c in range(4):
            z_ref[b, c, c * H : (c + 1) * H] += ridge
    inverses = [invert(z_ref[b, 0, :H]) for b in range(NBOX)]
    for kb in range(4):
        rows = slice(kb * H, (kb + 1) * H)
        below = slice((kb + 1) * H, 512)
        following = slice((kb + 1) * H, (kb + 2) * H)
        spread = [expand(x) for x in inverses]
        blocks, others = [], []
        for b in range(NBOX):
            blocks.append(z_ref[b, kb, below])
            others.append({c: expand(z_ref[b, c, rows]) for c in range(4) if c != kb})
        if kb < 3:
            inverses = []
            for b in range(NBOX):
                top = dot(blocks[b][:H], spread[b], precision=highest)
                inverses.append(
                    invert(z_ref[b, kb + 1, following] - dot(top, others[b][kb + 1], precision=highest))
                )
        for b in range(NBOX):
            block = dot(blocks[b], spread[b], precision=highest)
            z_ref[b, kb, below] = block
            step = dot(block, jnp.concatenate(list(others[b].values()), axis=1), precision=highest)
            for i, c in enumerate(others[b]):
                z_ref[b, c, below] -= step[:, 2 * H * i : 2 * H * (i + 1)]


def far_pairs(
    boxes_ref, places_ref, before_ref, after_ref, shared0, shared1, shared2, shared3, z_in, source_ref,
    interp_ref, x_out, to_before_ref, to_after_ref,
    list_ref, point_ref, rhs_ref, low_ref, rest_ref, rest_low_ref, main0_ref, side0_ref, main1_ref, side1_ref,
    z_ref, q_ref, x_ref, update_ref, proxy_ref,
):
    col = lax.axis_index("col")
    shared = (shared0, shared1, shared2, shared3)
    list_pairs(boxes_ref, list_ref, False)
    for slot in range(2):
        point_ref[slot] = ordered(before_ref[slot])
        point_ref[2 + slot] = ordered(after_ref[slot])
    for d in range(4):
        data = shared[d][...]
        points = jnp.concatenate([jnp.where(row_ids(S)[:4] < 3, 3.0 * data, 0.0), jnp.zeros_like(data)], axis=0)
        proxy_ref[d] = features(points, False).astype(bf16)
    put_pivots(q_ref, shared)
    z_ref[...] = z_in[...]
    even, odd = (main0_ref, side0_ref), (main1_ref, side1_ref)

    def far_slot(b, k):
        step, place = pair_step(boxes_ref, b, k)
        return (step & 2) + place

    pair_tiles(
        boxes_ref, places_ref, list_ref, source_ref, lambda b, k: point_ref[far_slot(b, k)],
        (rhs_ref, low_ref, rest_ref, rest_low_ref), z_ref, even, odd,
    )

    @pl.loop(0, 4)
    def _(i):
        b = i >> 1
        b_last = jnp.where(i == 0, list_ref[NBR - 1] >> 3, (i - 1) >> 1)
        d = 2 * (i & 1)
        tile(source_ref, b, proxy_ref[d], even, None, z_ref, b_last, odd)
        tile(source_ref, b, proxy_ref[d + 1], odd, None, z_ref, b, even)

    for piece in PIECES.values():
        gram_piece(z_ref, 1, odd, piece)
    solve(z_ref)
    for b in range(NBOX):
        x = jnp.concatenate([z_ref[b, c, S:] for c in range(4)], axis=1)
        x_out[b] = x
        put_x(x_ref, x, b)
        mine = [z_ref[b, c, pl.ds(pl.multiple_of(S + col * H, H), H)] for c in range(4)]
        for part in range(2):
            interp_ref[b, part] = jnp.concatenate([m[:, part * H : (part + 1) * H] for m in mine], axis=1)

    update_ref[...] = jnp.zeros_like(update_ref)
    for i in range(NBR):
        p = list_ref[i]
        b, k = p >> 3, p & 7
        rest = rest_ref[i].astype(f32) + rest_low_ref[i].astype(f32)
        update_ref[far_slot(b, k)] -= pair_update(x_ref, q_ref, b, rhs_ref[i], low_ref[i], rest)
    for slot in range(2):
        to_before_ref[slot] = pltpu.roll(update_ref[slot], H * col, 1)
        to_after_ref[slot] = pltpu.roll(update_ref[2 + slot], H * col, 1)


def own_updates(
    boxes_ref, shared0, shared1, shared2, shared3, x_in, rhs_in, low_in, rest_in, rest_low_in,
    update_ref,
    list_ref, rhs_ref, low_ref, rest_ref, rest_low_ref, q_ref, x_ref, sum_ref, sems,
):
    held = (rhs_ref, low_ref, rest_ref, rest_low_ref)
    given = (rhs_in, low_in, rest_in, rest_low_in)
    copies = [
        [pltpu.make_async_copy(src.at[i], dst.at[i], sems.at[i, n]) for n, (src, dst) in enumerate(zip(given, held))]
        for i in range(NBR)
    ]
    for group in copies:
        for copy in group:
            copy.start()
    list_pairs(boxes_ref, list_ref, True)
    put_pivots(q_ref, (shared0, shared1, shared2, shared3))
    for b in range(NBOX):
        put_x(x_ref, x_in[b], b)
    sum_ref[...] = jnp.zeros_like(sum_ref)
    for i in range(NBR):
        for copy in copies[i]:
            copy.wait()
        p = list_ref[i]
        b, k = p >> 3, p & 7
        rest = rest_ref[i].astype(f32) + rest_low_ref[i].astype(f32)
        sum_ref[pair_step(boxes_ref, b, k)[1]] -= pair_update(x_ref, q_ref, b, rhs_ref[i], low_ref[i], rest)
    for slot in range(2):
        update_ref[slot] = pltpu.roll(sum_ref[slot], H * lax.axis_index("col"), 1)


def on_device(
    box_points, proxy_directions, point_order, neighbour_boxes, neighbour_places, pivot_inverse
):
    count = lax.axis_size("box")
    forward = [(i, (i + 1) % count) for i in range(count)]
    backward = [((i + 1) % count, i) for i in range(count)]
    own = jnp.concatenate([box_points, point_order.astype(f32)[:, None, :]], axis=1)
    before = lax.ppermute(own, "box", forward)
    after = lax.ppermute(own, "box", backward)
    mine = jnp.concatenate([proxy_directions, pivot_inverse.reshape(1, S)], axis=0)
    cols = lax.axis_size("col")
    shared = [mine] + [
        lax.ppermute(mine, "col", [(i, (i + shift) % cols) for i in range(cols)]) for shift in range(1, 4)
    ]
    smem = pl.BlockSpec(memory_space=pltpu.SMEM)
    vmem = pl.BlockSpec(memory_space=pltpu.VMEM)
    hbm = pl.BlockSpec(memory_space=pl.ANY)
    params = pltpu.CompilerParams(vmem_limit_bytes=56 * 1024 * 1024)
    list_scratch = pltpu.SMEM((NBR,), jnp.int32)
    kept_shapes = ((NBR, 512, 512), (NBR, 512, 512), (NBR, S, 512), (NBR, S, 512))
    kept = [pltpu.VMEM(shape, bf16) for shape in kept_shapes]
    turns = [pltpu.VMEM(shape, bf16) for shape in ((512, 512), (S, 512), (512, 512), (S, 512))]
    z_shape = (NBOX, 4, 512, 2 * H)
    q_scratch = pltpu.VMEM((NBOX, 2, S, 128), f32)
    x_scratch = pltpu.VMEM((NBOX, 512, 512), bf16)
    z, source, *held = pl.pallas_call(
        own_tiles,
        out_shape=[jax.ShapeDtypeStruct(z_shape, f32), jax.ShapeDtypeStruct((NBOX, 512, 48), bf16)]
        + [jax.ShapeDtypeStruct(shape, bf16) for shape in kept_shapes],
        in_specs=[smem, smem, vmem],
        out_specs=[vmem, vmem] + [hbm] * 4,
        scratch_shapes=[list_scratch, pltpu.VMEM((NBOX, 8, 512), f32)] + kept + turns + [pltpu.SemaphoreType.DMA((NBR, 4))],
        compiler_params=params,
        cost_estimate=pl.CostEstimate(flops=20_000_000_000, bytes_accessed=16_000_000, transcendentals=2_000_000),
        name="own_tiles",
    )(neighbour_boxes, neighbour_places, own)
    rows = jax.ShapeDtypeStruct((NBOX, 2 * H, S), f32)
    interpolation, x, to_before, to_after = pl.pallas_call(
        far_pairs,
        out_shape=[jax.ShapeDtypeStruct((NBOX, 2, H, S), f32), jax.ShapeDtypeStruct((NBOX, S, 512), f32), rows, rows],
        in_specs=[smem, smem] + [vmem] * 8,
        out_specs=[vmem] * 4,
        scratch_shapes=[list_scratch, pltpu.VMEM((4, 8, 512), f32)] + kept + turns
        + [pltpu.VMEM(z_shape, f32), q_scratch, x_scratch, pltpu.VMEM((4, 2 * H, S), f32), pltpu.VMEM((4, 48, S), bf16)],
        compiler_params=params,
        cost_estimate=pl.CostEstimate(flops=60_000_000_000, bytes_accessed=8_000_000, transcendentals=4_000_000),
        name="far_pairs",
    )(neighbour_boxes, neighbour_places, before, after, *shared, z, source)
    from_before = lax.ppermute(to_after, "box", forward)
    from_after = lax.ppermute(to_before, "box", backward)
    update = pl.pallas_call(
        own_updates,
        out_shape=rows,
        in_specs=[smem] + [vmem] * 5 + [hbm] * 4,
        out_specs=vmem,
        scratch_shapes=[list_scratch] + kept
        + [q_scratch, x_scratch, pltpu.VMEM((NBOX, 2 * H, S), f32), pltpu.SemaphoreType.DMA((NBR, 4))],
        compiler_params=params,
        cost_estimate=pl.CostEstimate(flops=10_000_000_000, bytes_accessed=16_000_000, transcendentals=0),
        name="own_updates",
    )(neighbour_boxes, *shared, x, *held)
    return interpolation.transpose(0, 1, 3, 2), (update + from_before + from_after).reshape(NBOX, 2, H, S)


def solution(mesh):
    placed = (
        P("box", None, None),
        P(None, "col"),
        P("box", None),
        P("box", None),
        P("box", None),
        P("box", None, "col"),
    )
    return jax.shard_map(
        on_device,
        mesh=mesh,
        in_specs=placed,
        out_specs=(P("box", None, None, "col"), P("box", None, "col", None)),
        check_vma=False,
    )
```

```python
import math

import jax
import jax.numpy as jnp
import numpy as np
from jax import lax
from jax.experimental import pallas as pl
from jax.experimental.pallas import tpu as pltpu
from jax.sharding import PartitionSpec as P

S = 256
H = 64
NBR = 8
NBOX = 2
f32 = jnp.float32
bf16 = jnp.bfloat16
softening = 0.05
ridge_share = 0.05


def chebyshev_fit(function, count):
    nodes = 0.125 + 0.125 * np.cos(np.pi * (np.arange(256) + 0.5) / 256)
    fit = np.polynomial.chebyshev.Chebyshev.fit(nodes, function(np.sqrt(nodes)), count - 1, domain=[0, 0.25])
    return [float(c) for c in fit.convert(kind=np.polynomial.Polynomial).coef]


SIN_COEF = chebyshev_fit(lambda g: np.sin(np.pi * g) / (g * math.sqrt(math.pi)), 4)
COS_COEF = chebyshev_fit(lambda g: np.cos(np.pi * g) / math.sqrt(math.pi), 5)


def horner(z, coef):
    out = coef[-1]
    for c in coef[-2::-1]:
        out = out * z + c
    return out


def split2(x):
    high = x.astype(bf16)
    return high, (x - high.astype(f32)).astype(bf16)


def split3(x):
    high = x.astype(bf16).astype(f32)
    rest = x - high
    middle = rest.astype(bf16).astype(f32)
    return high, middle, (rest - middle).astype(bf16).astype(f32)


def dot(a, b, rhs_transposed=False, precision=None):
    dims = (((1,), (1 if rhs_transposed else 0,)), ((), ()))
    return lax.dot_general(a, b, dims, precision=precision, preferred_element_type=f32)


def turned(x):
    swapped = pltpu.roll(x, x.shape[1] // 2, 1)
    lane = lax.broadcasted_iota(jnp.int32, x.shape, 1)
    return jnp.where(lane < x.shape[1] // 2, -swapped, swapped)


def expand(x):
    return jnp.concatenate([x, turned(x)], axis=0)


def evaluate(v):
    inv = lax.rsqrt(v)
    turns = v * inv
    g = turns - jnp.round(turns)
    z = g * g
    s = g * horner(z, SIN_COEF)
    c = horner(z, COS_COEF)
    return inv * (1.0 / (2.0 * math.pi) - s * s), inv * (s * c)


def times(a, b):
    return a[0] * b[0] - a[1] * b[1], a[0] * b[1] + a[1] * b[0]


def invert(w):
    shape = (8, 2 * H)
    row_id = lax.broadcasted_iota(jnp.int32, shape, 0)
    lane_id = lax.broadcasted_iota(jnp.int32, shape, 1)
    line_id = lax.broadcasted_iota(jnp.int32, (1, 2 * H), 1)
    groups = [w[8 * g : 8 * g + 8] for g in range(H // 8)]
    for p in range(H // 8):
        columns = [
            [
                tuple(jnp.broadcast_to(w_g[:, at : at + 1], shape) for at in (8 * p + j, H + 8 * p + j))
                for j in range(8)
            ]
            for w_g in groups
        ]
        rows = groups[p]
        rows_t = turned(rows)
        small = list(columns[p])
        for j in range(8):
            at = 8 * p + j
            pivot = 1.0 / small[j][0][j : j + 1]
            row = jnp.where(line_id == at, pivot, jnp.where(line_id == H + at, 0.0, rows[j : j + 1] * pivot))
            row_t = jnp.where(line_id == H + at, pivot, jnp.where(line_id == at, 0.0, rows_t[j : j + 1] * pivot))
            here = row_id == j
            re = jnp.where(here, -1.0, small[j][0])
            im = jnp.where(here, 0.0, small[j][1])
            out = here | (lane_id == at) | (lane_id == H + at)
            rows = jnp.where(out, 0.0, rows) - re * row - im * row_t
            rows_t = jnp.where(out, 0.0, rows_t) - re * row_t + im * row
            for l in range(j + 1, 8):
                factor = tuple(x[j : j + 1] * pivot for x in small[l])
                step = times((re, im), factor)
                small[l] = tuple(jnp.where(here, 0.0, x) - y for x, y in zip(small[l], step))
        panel = ((lane_id >= 8 * p) & (lane_id < 8 * p + 8)) | ((lane_id >= H + 8 * p) & (lane_id < H + 8 * p + 8))
        for g in range(H // 8):
            if g == p:
                groups[g] = rows
                continue
            terms = [
                columns[g][j][0] * rows[j : j + 1] + columns[g][j][1] * rows_t[j : j + 1] for j in range(8)
            ]
            while len(terms) > 1:
                terms = [x + y for x, y in zip(terms[::2], terms[1::2])]
            groups[g] = jnp.where(panel, 0.0, groups[g]) - terms[0]
    return jnp.concatenate(groups, axis=0)


def on_diagonals(shape):
    return lax.broadcasted_iota(jnp.int32, shape, 0) == lax.broadcasted_iota(jnp.int32, shape, 1)


def row_ids(width):
    return lax.broadcasted_iota(jnp.int32, (8, width), 0)


def ordered(data):
    pick = (lax.broadcasted_iota(jnp.int32, (512, 512), 0).astype(f32) == data[3:4]).astype(bf16)
    parts = split3(2.0 * data - 1.0)
    got = dot(jnp.concatenate(parts + (jnp.zeros_like(data),), axis=0).astype(bf16), pick)
    points = jnp.where(row_ids(512)[:4] < 3, (got[0:4] + got[4:8]) + got[8:12], 0.0)
    return jnp.concatenate([points, jnp.zeros_like(points)], axis=0)


def features(points, is_source):
    rows = row_ids(points.shape[1])
    square = jnp.sum(points * points, axis=0, keepdims=True)
    if is_source:
        square = square + 4.0 * softening * softening
        high, middle, low = split3(points)
        groups = (high, high, middle, high, low, middle)
    else:
        high, middle, low = split3(-2.0 * points)
        groups = (high, middle, high, low, high, middle)
    own_row, other_row = (4, 3) if is_source else (3, 4)
    squares = split3(square)
    out = [
        jnp.where(rows == own_row, squares[i], jnp.where(rows == other_row, 1.0, group)) if i < 3 else group
        for i, group in enumerate(groups)
    ]
    return jnp.concatenate(out, axis=0)


def pair_step(boxes_ref, b, k):
    me, total = lax.axis_index("box"), lax.axis_size("box")
    box = boxes_ref[b, k]
    return lax.rem((box >> 1) - me + 1 + total, total), box & 1


def list_pairs(boxes_ref, list_ref, own):
    found = jnp.int32(0)
    for p in range(NBOX * NBR):
        step, _ = pair_step(boxes_ref, p // NBR, p % NBR)
        fits = (step == 1) if own else (step != 1)

        @pl.when(fits & (found < NBR))
        def _():
            list_ref[found] = p

        found = found + fits.astype(jnp.int32)


def pair_features(places_ref, points, b, k):
    code = places_ref[b, k]
    code = code + (code >= 13).astype(jnp.int32)
    rows = row_ids(512)
    move = jnp.zeros((8, 512), f32)
    for axis, digit in enumerate((code // 9, code // 3 % 3, code % 3)):
        move = jnp.where(rows == axis, (2 * digit - 2).astype(f32), move)
    got = features(points + move, False)
    back = lax.rem(S - H * lax.axis_index("col"), S)
    return pltpu.roll(got[:, :S], back, 1).astype(bf16), got[:, S:].astype(bf16)


def gram_piece(z_ref, b, in_refs, piece):
    main_ref, side_ref = in_refs
    half, n0 = piece
    if half == 0:
        left = jnp.concatenate([main_ref[2 * H * g : 2 * H * g + H] for g in range(4)], axis=0)
    else:
        left = side_ref[...]
    got = dot(left, main_ref[n0 : n0 + S], rhs_transposed=True)
    for i in range(2):
        z_ref[b, n0 // 128 + i, S * half : S * (half + 1)] += got[:, 2 * H * i : 2 * H * (i + 1)]


PIECES = {0: (0, 0), 2: (1, 0), 4: (0, S), 6: (1, S)}


def tile(source_ref, b, features_t, out_refs, kept, z_ref, b_in, in_refs):
    main_ref, side_ref = out_refs
    for g in range(8):
        if g in PIECES:
            gram_piece(z_ref, b_in, in_refs, PIECES[g])
        re, im = evaluate(dot(source_ref[b, g * H : (g + 1) * H], features_t))
        re_high, im_high = re.astype(bf16), im.astype(bf16)
        high = jnp.concatenate([re_high, im_high], axis=1)
        if g < 4:
            span = slice(2 * H * g, 2 * H * (g + 1))
            high = jnp.concatenate([high, jnp.concatenate([-im_high, re_high], axis=1)], axis=0)
            main_ref[span] = high
        else:
            span = slice(H * (g - 4), H * (g - 3))
            side_ref[span] = high
        if kept is None:
            continue
        i, rhs_ref, low_ref, rest_ref, rest_low_ref = kept
        re_low = (re - re_high.astype(f32)).astype(bf16)
        im_low = (im - im_high.astype(f32)).astype(bf16)
        low = jnp.concatenate([re_low, im_low], axis=1)
        if g < 4:
            low = jnp.concatenate([low, jnp.concatenate([-im_low, re_low], axis=1)], axis=0)
            rhs_ref[i, span] = high
            low_ref[i, span] = low
        else:
            rest_ref[i, span] = high
            rest_low_ref[i, span] = low


def pair_tiles(boxes_ref, places_ref, list_ref, source_ref, points_of, kept, z_ref, even, odd, after_each=None):
    for ref in odd:
        ref[...] = jnp.zeros_like(ref)

    @pl.loop(0, NBR)
    def _(i):
        p = list_ref[i]
        b_last = list_ref[jnp.maximum(i - 1, 0)] >> 3
        b, k = p >> 3, p & 7
        skeleton, redundant = pair_features(places_ref, points_of(b, k), b, k)
        tile(source_ref, b, skeleton, even, (i,) + kept, z_ref, b_last, odd)
        if after_each is not None:
            after_each(i)
        tile(source_ref, b, redundant, odd, None, z_ref, b, even)


def put_pivots(q_ref, shared):
    col = lax.axis_index("col")
    flat = jnp.concatenate([ref[3:4] for ref in shared] + [jnp.zeros((4, S), f32)], axis=0).T
    for b in range(NBOX):
        for part in range(2):
            first = (2 * b + part) * H
            for shift in range(4):
                rows = pl.ds(pl.multiple_of(lax.rem(col - shift + 4, 4) * H, H), H)
                q_ref[b, part, rows] = jnp.broadcast_to(flat[first : first + H, shift : shift + 1], (H, 128))


def pair_updates(boxes_ref, list_ref, x_ref, q_ref, held, block_ref, sum_ref, place_of, before_each=None):
    rhs_ref, low_ref, rest_ref, rest_low_ref = held

    def block_half(i, part):
        b = list_ref[i] >> 3
        lanes = slice(S * part, S * (part + 1))
        x_both = x_ref[b]
        both = dot(x_both, rhs_ref[i, :, lanes])
        rest = rest_ref[i, :, lanes].astype(f32) + rest_low_ref[i, :, lanes].astype(f32)
        block_ref[i % 2, S * part : S * (part + 1)] = rest - (
            (both[:S] + both[S:]) + dot(x_both[:S], low_ref[i, :, lanes])
        )

    def weigh(i):
        b = list_ref[i] >> 3
        first = jnp.concatenate([block_ref[i % 2, :S, :H], block_ref[i % 2, S:, :H]], axis=1)
        weighted = (q_ref[b, 0] * first + q_ref[b, 1] * turned(first)).T
        left = jnp.concatenate([weighted, jnp.concatenate([-weighted[H:], weighted[:H]], axis=0)], axis=1)
        return split2(left)

    def finish(i, left):
        high, low = left
        right_high, right_low = split2(block_ref[i % 2])
        got = dot(jnp.concatenate([high, low], axis=0), right_high)
        p = list_ref[i]
        sum_ref[place_of(p >> 3, p & 7)] -= (got[: 2 * H] + got[2 * H :]) + dot(high, right_low)

    for i in range(NBR + 1):
        if i < NBR:
            if before_each is not None:
                before_each(i)
            block_half(i, 0)
        if i > 0:
            left = weigh(i - 1)
        if i < NBR:
            block_half(i, 1)
        if i > 0:
            finish(i - 1, left)


def put_x(x_ref, x, b):
    high, low = split2(x)
    x_ref[b, :S] = high
    x_ref[b, S:] = low


def gather_inputs(points_ref, directions_ref, order_ref, pivot_ref, own_ref, mine_ref):
    for b in range(NBOX):
        own_ref[b, 0:3] = points_ref[b]
        own_ref[b, 3:4] = order_ref[b : b + 1].astype(f32)
        for part in range(2):
            first = (2 * b + part) * H
            mine_ref[3:4, first : first + H] = pivot_ref[b, part : part + 1]
    mine_ref[0:3] = directions_ref[...]


def own_tiles(
    boxes_ref, places_ref, own_ref,
    z_ref, source_ref, rhs_out, low_out, rest_out, rest_low_out,
    list_ref, point_ref, rhs_ref, low_ref, rest_ref, rest_low_ref, main0_ref, side0_ref, main1_ref, side1_ref, sems,
):
    list_pairs(boxes_ref, list_ref, True)
    for b in range(NBOX):
        point_ref[b] = ordered(own_ref[b])
        source_ref[b] = features(point_ref[b], True).T.astype(bf16)
    z_ref[...] = jnp.zeros_like(z_ref)
    even, odd = (main0_ref, side0_ref), (main1_ref, side1_ref)
    kept = (rhs_ref, low_ref, rest_ref, rest_low_ref)
    outs = (rhs_out, low_out, rest_out, rest_low_out)

    def copies(i):
        return [pltpu.make_async_copy(src.at[i], dst.at[i], sems.at[i, n]) for n, (src, dst) in enumerate(zip(kept, outs))]

    def start(i):
        for copy in copies(i):
            copy.start()

    pair_tiles(
        boxes_ref, places_ref, list_ref, source_ref,
        lambda b, k: point_ref[pair_step(boxes_ref, b, k)[1]],
        kept, z_ref, even, odd, start,
    )
    for piece in PIECES.values():
        gram_piece(z_ref, list_ref[NBR - 1] >> 3, odd, piece)
    for i in range(NBR):
        for copy in copies(i):
            copy.wait()


def solve(z_ref):
    highest = lax.Precision.HIGHEST
    on_diagonal = on_diagonals((H, 2 * H))
    for b in range(NBOX):
        total = jnp.zeros((H, 2 * H), f32)
        for c in range(4):
            total = total + jnp.where(on_diagonal, z_ref[b, c, c * H : (c + 1) * H], 0.0)
        trace = jnp.sum(jnp.sum(total, axis=0, keepdims=True), axis=1, keepdims=True)
        ridge = jnp.where(on_diagonal, ridge_share * trace / S, 0.0)
        for c in range(4):
            z_ref[b, c, c * H : (c + 1) * H] += ridge
    inverses = [invert(z_ref[b, 0, :H]) for b in range(NBOX)]
    for kb in range(4):
        rows = slice(kb * H, (kb + 1) * H)
        below = slice((kb + 1) * H, 512)
        following = slice((kb + 1) * H, (kb + 2) * H)
        spread = [expand(x) for x in inverses]
        blocks, others = [], []
        for b in range(NBOX):
            blocks.append(z_ref[b, kb, below])
            others.append({c: expand(z_ref[b, c, rows]) for c in range(4) if c != kb})
        if kb < 3:
            inverses = []
            for b in range(NBOX):
                top = dot(blocks[b][:H], spread[b], precision=highest)
                inverses.append(
                    invert(z_ref[b, kb + 1, following] - dot(top, others[b][kb + 1], precision=highest))
                )
        for b in range(NBOX):
            block = dot(blocks[b], spread[b], precision=highest)
            z_ref[b, kb, below] = block
            step = dot(block, jnp.concatenate(list(others[b].values()), axis=1), precision=highest)
            for i, c in enumerate(others[b]):
                z_ref[b, c, below] -= step[:, 2 * H * i : 2 * H * (i + 1)]


def far_pairs(
    boxes_ref, places_ref, before_ref, after_ref, shared0, shared1, shared2, shared3, z_in, source_ref,
    interp_ref, x_out, to_before_ref, to_after_ref,
    list_ref, point_ref, rhs_ref, low_ref, rest_ref, rest_low_ref, main0_ref, side0_ref, main1_ref, side1_ref,
    z_ref, q_ref, x_ref, update_ref, proxy_ref, block_ref,
):
    col = lax.axis_index("col")
    shared = (shared0, shared1, shared2, shared3)
    list_pairs(boxes_ref, list_ref, False)
    for slot in range(2):
        point_ref[slot] = ordered(before_ref[slot])
        point_ref[2 + slot] = ordered(after_ref[slot])
    for d in range(4):
        data = shared[d][...]
        points = jnp.concatenate([jnp.where(row_ids(S)[:4] < 3, 3.0 * data, 0.0), jnp.zeros_like(data)], axis=0)
        proxy_ref[d] = features(points, False).astype(bf16)
    put_pivots(q_ref, shared)
    z_ref[...] = z_in[...]
    even, odd = (main0_ref, side0_ref), (main1_ref, side1_ref)

    def far_slot(b, k):
        step, place = pair_step(boxes_ref, b, k)
        return (step & 2) + place

    pair_tiles(
        boxes_ref, places_ref, list_ref, source_ref, lambda b, k: point_ref[far_slot(b, k)],
        (rhs_ref, low_ref, rest_ref, rest_low_ref), z_ref, even, odd,
    )

    @pl.loop(0, 4)
    def _(i):
        b = i >> 1
        b_last = jnp.where(i == 0, list_ref[NBR - 1] >> 3, (i - 1) >> 1)
        d = 2 * (i & 1)
        tile(source_ref, b, proxy_ref[d], even, None, z_ref, b_last, odd)
        tile(source_ref, b, proxy_ref[d + 1], odd, None, z_ref, b, even)

    for piece in PIECES.values():
        gram_piece(z_ref, 1, odd, piece)
    solve(z_ref)
    for b in range(NBOX):
        x = jnp.concatenate([z_ref[b, c, S:] for c in range(4)], axis=1)
        x_out[b] = x
        put_x(x_ref, x, b)
        mine = [z_ref[b, c, pl.ds(pl.multiple_of(S + col * H, H), H)] for c in range(4)]
        for part in range(2):
            interp_ref[b, part] = jnp.concatenate([m[:, part * H : (part + 1) * H] for m in mine], axis=1)

    update_ref[...] = jnp.zeros_like(update_ref)
    held = (rhs_ref, low_ref, rest_ref, rest_low_ref)
    pair_updates(boxes_ref, list_ref, x_ref, q_ref, held, block_ref, update_ref, far_slot)
    for slot in range(2):
        to_before_ref[slot] = pltpu.roll(update_ref[slot], H * col, 1)
        to_after_ref[slot] = pltpu.roll(update_ref[2 + slot], H * col, 1)


def own_updates(
    boxes_ref, shared0, shared1, shared2, shared3, x_in, rhs_in, low_in, rest_in, rest_low_in,
    update_ref,
    list_ref, rhs_ref, low_ref, rest_ref, rest_low_ref, q_ref, x_ref, sum_ref, block_ref, sems,
):
    held = (rhs_ref, low_ref, rest_ref, rest_low_ref)
    given = (rhs_in, low_in, rest_in, rest_low_in)
    copies = [
        [pltpu.make_async_copy(src.at[i], dst.at[i], sems.at[i, n]) for n, (src, dst) in enumerate(zip(given, held))]
        for i in range(NBR)
    ]
    for group in copies:
        for copy in group:
            copy.start()
    list_pairs(boxes_ref, list_ref, True)
    put_pivots(q_ref, (shared0, shared1, shared2, shared3))
    for b in range(NBOX):
        put_x(x_ref, x_in[b], b)
    sum_ref[...] = jnp.zeros_like(sum_ref)

    def arrive(i):
        for copy in copies[i]:
            copy.wait()

    pair_updates(
        boxes_ref, list_ref, x_ref, q_ref, held, block_ref, sum_ref, lambda b, k: pair_step(boxes_ref, b, k)[1], arrive
    )
    for slot in range(2):
        update_ref[slot] = pltpu.roll(sum_ref[slot], H * lax.axis_index("col"), 1)


def on_device(
    box_points, proxy_directions, point_order, neighbour_boxes, neighbour_places, pivot_inverse
):
    count = lax.axis_size("box")
    forward = [(i, (i + 1) % count) for i in range(count)]
    backward = [((i + 1) % count, i) for i in range(count)]
    smem = pl.BlockSpec(memory_space=pltpu.SMEM)
    vmem = pl.BlockSpec(memory_space=pltpu.VMEM)
    own, mine = pl.pallas_call(
        gather_inputs,
        out_shape=[jax.ShapeDtypeStruct((NBOX, 4, 512), f32), jax.ShapeDtypeStruct((4, S), f32)],
        in_specs=[vmem] * 4,
        out_specs=[vmem] * 2,
        name="gather_inputs",
    )(box_points, proxy_directions, point_order, pivot_inverse)
    before = lax.ppermute(own, "box", forward)
    after = lax.ppermute(own, "box", backward)
    cols = lax.axis_size("col")
    shared = [mine] + [
        lax.ppermute(mine, "col", [(i, (i + shift) % cols) for i in range(cols)]) for shift in range(1, 4)
    ]
    hbm = pl.BlockSpec(memory_space=pl.ANY)
    params = pltpu.CompilerParams(vmem_limit_bytes=56 * 1024 * 1024)
    list_scratch = pltpu.SMEM((NBR,), jnp.int32)
    kept_shapes = ((NBR, 512, 512), (NBR, 512, 512), (NBR, S, 512), (NBR, S, 512))
    kept = [pltpu.VMEM(shape, bf16) for shape in kept_shapes]
    turns = [pltpu.VMEM(shape, bf16) for shape in ((512, 512), (S, 512), (512, 512), (S, 512))]
    z_shape = (NBOX, 4, 512, 2 * H)
    q_scratch = pltpu.VMEM((NBOX, 2, S, 128), f32)
    x_scratch = pltpu.VMEM((NBOX, 512, 512), bf16)
    z, source, *held = pl.pallas_call(
        own_tiles,
        out_shape=[jax.ShapeDtypeStruct(z_shape, f32), jax.ShapeDtypeStruct((NBOX, 512, 48), bf16)]
        + [jax.ShapeDtypeStruct(shape, bf16) for shape in kept_shapes],
        in_specs=[smem, smem, vmem],
        out_specs=[vmem, vmem] + [hbm] * 4,
        scratch_shapes=[list_scratch, pltpu.VMEM((NBOX, 8, 512), f32)] + kept + turns + [pltpu.SemaphoreType.DMA((NBR, 4))],
        compiler_params=params,
        cost_estimate=pl.CostEstimate(flops=20_000_000_000, bytes_accessed=16_000_000, transcendentals=2_000_000),
        name="own_tiles",
    )(neighbour_boxes, neighbour_places, own)
    rows = jax.ShapeDtypeStruct((NBOX, 2 * H, S), f32)
    interpolation, x, to_before, to_after = pl.pallas_call(
        far_pairs,
        out_shape=[jax.ShapeDtypeStruct((NBOX, 2, H, S), f32), jax.ShapeDtypeStruct((NBOX, S, 512), f32), rows, rows],
        in_specs=[smem, smem] + [vmem] * 8,
        out_specs=[vmem] * 4,
        scratch_shapes=[list_scratch, pltpu.VMEM((4, 8, 512), f32)] + kept + turns
        + [pltpu.VMEM(z_shape, f32), q_scratch, x_scratch, pltpu.VMEM((4, 2 * H, S), f32), pltpu.VMEM((4, 48, S), bf16), pltpu.VMEM((2, 512, S), f32)],
        compiler_params=params,
        cost_estimate=pl.CostEstimate(flops=60_000_000_000, bytes_accessed=8_000_000, transcendentals=4_000_000),
        name="far_pairs",
    )(neighbour_boxes, neighbour_places, before, after, *shared, z, source)
    from_before = lax.ppermute(to_after, "box", forward)
    from_after = lax.ppermute(to_before, "box", backward)
    update = pl.pallas_call(
        own_updates,
        out_shape=rows,
        in_specs=[smem] + [vmem] * 5 + [hbm] * 4,
        out_specs=vmem,
        scratch_shapes=[list_scratch] + kept
        + [q_scratch, x_scratch, pltpu.VMEM((NBOX, 2 * H, S), f32), pltpu.VMEM((2, 512, S), f32), pltpu.SemaphoreType.DMA((NBR, 4))],
        compiler_params=params,
        cost_estimate=pl.CostEstimate(flops=10_000_000_000, bytes_accessed=16_000_000, transcendentals=0),
        name="own_updates",
    )(neighbour_boxes, *shared, x, *held)
    return interpolation.transpose(0, 1, 3, 2), (update + from_before + from_after).reshape(NBOX, 2, H, S)


def solution(mesh):
    placed = (
        P("box", None, None),
        P(None, "col"),
        P("box", None),
        P("box", None),
        P("box", None),
        P("box", None, "col"),
    )
    return jax.shard_map(
        on_device,
        mesh=mesh,
        in_specs=placed,
        out_specs=(P("box", None, None, "col"), P("box", None, "col", None)),
        check_vma=False,
    )
```

```python
import math

import jax
import jax.numpy as jnp
import numpy as np
from jax import lax
from jax.experimental import pallas as pl
from jax.experimental.pallas import tpu as pltpu
from jax.sharding import PartitionSpec as P

S = 256
H = 64
NBR = 8
NBOX = 2
f32 = jnp.float32
bf16 = jnp.bfloat16
softening = 0.05
ridge_share = 0.05


def chebyshev_fit(function, count):
    nodes = 0.125 + 0.125 * np.cos(np.pi * (np.arange(256) + 0.5) / 256)
    fit = np.polynomial.chebyshev.Chebyshev.fit(nodes, function(np.sqrt(nodes)), count - 1, domain=[0, 0.25])
    return [float(c) for c in fit.convert(kind=np.polynomial.Polynomial).coef]


SIN_COEF = chebyshev_fit(lambda g: np.sin(np.pi * g) / (g * math.sqrt(math.pi)), 4)
COS_COEF = chebyshev_fit(lambda g: np.cos(np.pi * g) / math.sqrt(math.pi), 5)


def horner(z, coef):
    out = coef[-1]
    for c in coef[-2::-1]:
        out = out * z + c
    return out


def split2(x):
    high = x.astype(bf16)
    return high, (x - high.astype(f32)).astype(bf16)


def split3(x):
    high = x.astype(bf16).astype(f32)
    rest = x - high
    middle = rest.astype(bf16).astype(f32)
    return high, middle, (rest - middle).astype(bf16).astype(f32)


def dot(a, b, rhs_transposed=False, precision=None):
    dims = (((1,), (1 if rhs_transposed else 0,)), ((), ()))
    return lax.dot_general(a, b, dims, precision=precision, preferred_element_type=f32)


def turned(x):
    swapped = pltpu.roll(x, x.shape[1] // 2, 1)
    lane = lax.broadcasted_iota(jnp.int32, x.shape, 1)
    return jnp.where(lane < x.shape[1] // 2, -swapped, swapped)


def expand(x):
    return jnp.concatenate([x, turned(x)], axis=0)


def evaluate(v):
    inv = lax.rsqrt(v)
    turns = v * inv
    g = turns - jnp.round(turns)
    z = g * g
    s = g * horner(z, SIN_COEF)
    c = horner(z, COS_COEF)
    return inv * (1.0 / (2.0 * math.pi) - s * s), inv * (s * c)


def times(a, b):
    return a[0] * b[0] - a[1] * b[1], a[0] * b[1] + a[1] * b[0]


def invert(w):
    shape = (8, 2 * H)
    row_id = lax.broadcasted_iota(jnp.int32, shape, 0)
    lane_id = lax.broadcasted_iota(jnp.int32, shape, 1)
    line_id = lax.broadcasted_iota(jnp.int32, (1, 2 * H), 1)
    groups = [w[8 * g : 8 * g + 8] for g in range(H // 8)]
    for p in range(H // 8):
        columns = [
            [
                tuple(jnp.broadcast_to(w_g[:, at : at + 1], shape) for at in (8 * p + j, H + 8 * p + j))
                for j in range(8)
            ]
            for w_g in groups
        ]
        rows = groups[p]
        rows_t = turned(rows)
        small = list(columns[p])
        for j in range(8):
            at = 8 * p + j
            pivot = 1.0 / small[j][0][j : j + 1]
            row = jnp.where(line_id == at, pivot, jnp.where(line_id == H + at, 0.0, rows[j : j + 1] * pivot))
            row_t = jnp.where(line_id == H + at, pivot, jnp.where(line_id == at, 0.0, rows_t[j : j + 1] * pivot))
            here = row_id == j
            re = jnp.where(here, -1.0, small[j][0])
            im = jnp.where(here, 0.0, small[j][1])
            out = here | (lane_id == at) | (lane_id == H + at)
            rows = jnp.where(out, 0.0, rows) - re * row - im * row_t
            rows_t = jnp.where(out, 0.0, rows_t) - re * row_t + im * row
            for l in range(j + 1, 8):
                factor = tuple(x[j : j + 1] * pivot for x in small[l])
                step = times((re, im), factor)
                small[l] = tuple(jnp.where(here, 0.0, x) - y for x, y in zip(small[l], step))
        panel = ((lane_id >= 8 * p) & (lane_id < 8 * p + 8)) | ((lane_id >= H + 8 * p) & (lane_id < H + 8 * p + 8))
        for g in range(H // 8):
            if g == p:
                groups[g] = rows
                continue
            terms = [
                columns[g][j][0] * rows[j : j + 1] + columns[g][j][1] * rows_t[j : j + 1] for j in range(8)
            ]
            while len(terms) > 1:
                terms = [x + y for x, y in zip(terms[::2], terms[1::2])]
            groups[g] = jnp.where(panel, 0.0, groups[g]) - terms[0]
    return jnp.concatenate(groups, axis=0)


def on_diagonals(shape):
    return lax.broadcasted_iota(jnp.int32, shape, 0) == lax.broadcasted_iota(jnp.int32, shape, 1)


def row_ids(width):
    return lax.broadcasted_iota(jnp.int32, (8, width), 0)


def ordered(data):
    pick = (lax.broadcasted_iota(jnp.int32, (512, 512), 0).astype(f32) == data[3:4]).astype(bf16)
    parts = split3(2.0 * data - 1.0)
    got = dot(jnp.concatenate(parts + (jnp.zeros_like(data),), axis=0).astype(bf16), pick)
    points = jnp.where(row_ids(512)[:4] < 3, (got[0:4] + got[4:8]) + got[8:12], 0.0)
    return jnp.concatenate([points, jnp.zeros_like(points)], axis=0)


def features(points, is_source):
    rows = row_ids(points.shape[1])
    square = jnp.sum(points * points, axis=0, keepdims=True)
    if is_source:
        square = square + 4.0 * softening * softening
        high, middle, low = split3(points)
        groups = (high, high, middle, high, low, middle)
    else:
        high, middle, low = split3(-2.0 * points)
        groups = (high, middle, high, low, high, middle)
    own_row, other_row = (4, 3) if is_source else (3, 4)
    squares = split3(square)
    out = [
        jnp.where(rows == own_row, squares[i], jnp.where(rows == other_row, 1.0, group)) if i < 3 else group
        for i, group in enumerate(groups)
    ]
    return jnp.concatenate(out, axis=0)


def pair_step(boxes_ref, b, k):
    me, total = lax.axis_index("box"), lax.axis_size("box")
    box = boxes_ref[b, k]
    return lax.rem((box >> 1) - me + 1 + total, total), box & 1


def list_pairs(boxes_ref, list_ref, own):
    found = jnp.int32(0)
    for p in range(NBOX * NBR):
        step, _ = pair_step(boxes_ref, p // NBR, p % NBR)
        fits = (step == 1) if own else (step != 1)

        @pl.when(fits & (found < NBR))
        def _():
            list_ref[found] = p

        found = found + fits.astype(jnp.int32)


def pair_features(places_ref, points, b, k):
    code = places_ref[b, k]
    code = code + (code >= 13).astype(jnp.int32)
    rows = row_ids(512)
    move = jnp.zeros((8, 512), f32)
    for axis, digit in enumerate((code // 9, code // 3 % 3, code % 3)):
        move = jnp.where(rows == axis, (2 * digit - 2).astype(f32), move)
    got = features(points + move, False)
    back = lax.rem(S - H * lax.axis_index("col"), S)
    return pltpu.roll(got[:, :S], back, 1).astype(bf16), got[:, S:].astype(bf16)


def gram_piece(z_ref, b, in_refs, piece):
    main_ref, side_ref = in_refs
    half, n0 = piece
    if half == 0:
        left = jnp.concatenate([main_ref[2 * H * g : 2 * H * g + H] for g in range(4)], axis=0)
    else:
        left = side_ref[...]
    got = dot(left, main_ref[n0 : n0 + S], rhs_transposed=True)
    for i in range(2):
        z_ref[b, n0 // 128 + i, S * half : S * (half + 1)] += got[:, 2 * H * i : 2 * H * (i + 1)]


PIECES = {0: (0, 0), 2: (1, 0), 4: (0, S), 6: (1, S)}


def tile(source_ref, b, features_t, out_refs, kept, z_ref, b_in, in_refs):
    main_ref, side_ref = out_refs
    for g in range(8):
        if g in PIECES:
            gram_piece(z_ref, b_in, in_refs, PIECES[g])
        re, im = evaluate(dot(source_ref[b, g * H : (g + 1) * H], features_t))
        re_high, im_high = re.astype(bf16), im.astype(bf16)
        high = jnp.concatenate([re_high, im_high], axis=1)
        if g < 4:
            span = slice(2 * H * g, 2 * H * (g + 1))
            high = jnp.concatenate([high, jnp.concatenate([-im_high, re_high], axis=1)], axis=0)
            main_ref[span] = high
        else:
            span = slice(H * (g - 4), H * (g - 3))
            side_ref[span] = high
        if kept is None:
            continue
        i, rhs_ref, low_ref, rest_ref, rest_low_ref = kept
        re_low = (re - re_high.astype(f32)).astype(bf16)
        im_low = (im - im_high.astype(f32)).astype(bf16)
        low = jnp.concatenate([re_low, im_low], axis=1)
        if g < 4:
            low = jnp.concatenate([low, jnp.concatenate([-im_low, re_low], axis=1)], axis=0)
            rhs_ref[i, span] = high
            low_ref[i, span] = low
        else:
            rest_ref[i, span] = high
            rest_low_ref[i, span] = low


def pair_tiles(boxes_ref, places_ref, list_ref, source_ref, points_of, kept, z_ref, even, odd, after_each=None):
    for ref in odd:
        ref[...] = jnp.zeros_like(ref)

    @pl.loop(0, NBR)
    def _(i):
        p = list_ref[i]
        b_last = list_ref[jnp.maximum(i - 1, 0)] >> 3
        b, k = p >> 3, p & 7
        skeleton, redundant = pair_features(places_ref, points_of(b, k), b, k)
        tile(source_ref, b, skeleton, even, (i,) + kept, z_ref, b_last, odd)
        if after_each is not None:
            after_each(i)
        tile(source_ref, b, redundant, odd, None, z_ref, b, even)


def put_pivots(q_ref, shared):
    col = lax.axis_index("col")
    flat = jnp.concatenate([ref[3:4] for ref in shared] + [jnp.zeros((4, S), f32)], axis=0).T
    for b in range(NBOX):
        for part in range(2):
            first = (2 * b + part) * H
            for shift in range(4):
                rows = pl.ds(pl.multiple_of(lax.rem(col - shift + 4, 4) * H, H), H)
                q_ref[b, part, rows] = jnp.broadcast_to(flat[first : first + H, shift : shift + 1], (H, 128))


def pair_updates(boxes_ref, list_ref, x_ref, q_ref, held, block_ref, sum_ref, place_of, before_each=None):
    rhs_ref, low_ref, rest_ref, rest_low_ref = held

    def block_half(i, part):
        b = list_ref[i] >> 3
        lanes = slice(S * part, S * (part + 1))
        x_both = x_ref[b]
        both = dot(x_both, rhs_ref[i, :, lanes])
        rest = rest_ref[i, :, lanes].astype(f32) + rest_low_ref[i, :, lanes].astype(f32)
        block_ref[i % 2, S * part : S * (part + 1)] = rest - (
            (both[:S] + both[S:]) + dot(x_both[:S], low_ref[i, :, lanes])
        )

    def weigh(i):
        b = list_ref[i] >> 3
        first = jnp.concatenate([block_ref[i % 2, :S, :H], block_ref[i % 2, S:, :H]], axis=1)
        weighted = (q_ref[b, 0] * first + q_ref[b, 1] * turned(first)).T
        left = jnp.concatenate([weighted, jnp.concatenate([-weighted[H:], weighted[:H]], axis=0)], axis=1)
        return split2(left)

    def finish(i, left):
        high, low = left
        right_high, right_low = split2(block_ref[i % 2])
        got = dot(jnp.concatenate([high, low], axis=0), right_high)
        p = list_ref[i]
        sum_ref[place_of(p >> 3, p & 7)] -= (got[: 2 * H] + got[2 * H :]) + dot(high, right_low)

    for i in range(NBR + 1):
        if i < NBR:
            if before_each is not None:
                before_each(i)
            block_half(i, 0)
        if i > 0:
            left = weigh(i - 1)
        if i < NBR:
            block_half(i, 1)
        if i > 0:
            finish(i - 1, left)


def put_x(x_ref, x, b):
    high, low = split2(x)
    x_ref[b, :S] = high
    x_ref[b, S:] = low


def gather_inputs(points_ref, directions_ref, order_ref, pivot_ref, own_ref, mine_ref):
    for b in range(NBOX):
        for axis in range(3):
            own_ref[b, axis : axis + 1] = points_ref[axis, b : b + 1]
        own_ref[b, 3:4] = order_ref[b : b + 1].astype(f32)
        for part in range(2):
            first = (2 * b + part) * H
            mine_ref[3:4, first : first + H] = pivot_ref[b, part : part + 1]
    mine_ref[0:3] = directions_ref[...]


def own_tiles(
    boxes_ref, places_ref, own_ref,
    z_ref, source_ref, rhs_out, low_out, rest_out, rest_low_out,
    list_ref, point_ref, rhs_ref, low_ref, rest_ref, rest_low_ref, main0_ref, side0_ref, main1_ref, side1_ref, sems,
):
    list_pairs(boxes_ref, list_ref, True)
    for b in range(NBOX):
        point_ref[b] = ordered(own_ref[b])
        source_ref[b] = features(point_ref[b], True).T.astype(bf16)
    z_ref[...] = jnp.zeros_like(z_ref)
    even, odd = (main0_ref, side0_ref), (main1_ref, side1_ref)
    kept = (rhs_ref, low_ref, rest_ref, rest_low_ref)
    outs = (rhs_out, low_out, rest_out, rest_low_out)

    def copies(i):
        return [pltpu.make_async_copy(src.at[i], dst.at[i], sems.at[i, n]) for n, (src, dst) in enumerate(zip(kept, outs))]

    def start(i):
        for copy in copies(i):
            copy.start()

    pair_tiles(
        boxes_ref, places_ref, list_ref, source_ref,
        lambda b, k: point_ref[pair_step(boxes_ref, b, k)[1]],
        kept, z_ref, even, odd, start,
    )
    for piece in PIECES.values():
        gram_piece(z_ref, list_ref[NBR - 1] >> 3, odd, piece)
    for i in range(NBR):
        for copy in copies(i):
            copy.wait()


def solve(z_ref):
    highest = lax.Precision.HIGHEST
    on_diagonal = on_diagonals((H, 2 * H))
    for b in range(NBOX):
        total = jnp.zeros((H, 2 * H), f32)
        for c in range(4):
            total = total + jnp.where(on_diagonal, z_ref[b, c, c * H : (c + 1) * H], 0.0)
        trace = jnp.sum(jnp.sum(total, axis=0, keepdims=True), axis=1, keepdims=True)
        ridge = jnp.where(on_diagonal, ridge_share * trace / S, 0.0)
        for c in range(4):
            z_ref[b, c, c * H : (c + 1) * H] += ridge
    inverses = [invert(z_ref[b, 0, :H]) for b in range(NBOX)]
    for kb in range(4):
        rows = slice(kb * H, (kb + 1) * H)
        below = slice((kb + 1) * H, 512)
        following = slice((kb + 1) * H, (kb + 2) * H)
        spread = [expand(x) for x in inverses]
        blocks, others = [], []
        for b in range(NBOX):
            blocks.append(z_ref[b, kb, below])
            others.append({c: expand(z_ref[b, c, rows]) for c in range(4) if c != kb})
        if kb < 3:
            inverses = []
            for b in range(NBOX):
                top = dot(blocks[b][:H], spread[b], precision=highest)
                inverses.append(
                    invert(z_ref[b, kb + 1, following] - dot(top, others[b][kb + 1], precision=highest))
                )
        for b in range(NBOX):
            block = dot(blocks[b], spread[b], precision=highest)
            z_ref[b, kb, below] = block
            step = dot(block, jnp.concatenate(list(others[b].values()), axis=1), precision=highest)
            for i, c in enumerate(others[b]):
                z_ref[b, c, below] -= step[:, 2 * H * i : 2 * H * (i + 1)]


def far_pairs(
    boxes_ref, places_ref, before_ref, after_ref, shared0, shared1, shared2, shared3, z_in, source_ref,
    interp_ref, x_ref, to_before_ref, to_after_ref,
    list_ref, point_ref, rhs_ref, low_ref, rest_ref, rest_low_ref, main0_ref, side0_ref, main1_ref, side1_ref,
    z_ref, q_ref, update_ref, proxy_ref, block_ref, sem,
):
    col = lax.axis_index("col")
    shared = (shared0, shared1, shared2, shared3)
    bring = pltpu.make_async_copy(z_in, z_ref, sem)
    bring.start()
    list_pairs(boxes_ref, list_ref, False)
    for slot in range(2):
        point_ref[slot] = ordered(before_ref[slot])
        point_ref[2 + slot] = ordered(after_ref[slot])
    for d in range(4):
        data = shared[d][...]
        points = jnp.concatenate([jnp.where(row_ids(S)[:4] < 3, 3.0 * data, 0.0), jnp.zeros_like(data)], axis=0)
        proxy_ref[d] = features(points, False).astype(bf16)
    put_pivots(q_ref, shared)
    bring.wait()
    even, odd = (main0_ref, side0_ref), (main1_ref, side1_ref)

    def far_slot(b, k):
        step, place = pair_step(boxes_ref, b, k)
        return (step & 2) + place

    pair_tiles(
        boxes_ref, places_ref, list_ref, source_ref, lambda b, k: point_ref[far_slot(b, k)],
        (rhs_ref, low_ref, rest_ref, rest_low_ref), z_ref, even, odd,
    )

    @pl.loop(0, 4)
    def _(i):
        b = i >> 1
        b_last = jnp.where(i == 0, list_ref[NBR - 1] >> 3, (i - 1) >> 1)
        d = 2 * (i & 1)
        tile(source_ref, b, proxy_ref[d], even, None, z_ref, b_last, odd)
        tile(source_ref, b, proxy_ref[d + 1], odd, None, z_ref, b, even)

    for piece in PIECES.values():
        gram_piece(z_ref, 1, odd, piece)
    solve(z_ref)
    for b in range(NBOX):
        x = jnp.concatenate([z_ref[b, c, S:] for c in range(4)], axis=1)
        put_x(x_ref, x, b)
        mine = [z_ref[b, c, pl.ds(pl.multiple_of(S + col * H, H), H)] for c in range(4)]
        for part in range(2):
            interp_ref[b, part] = jnp.concatenate([m[:, part * H : (part + 1) * H] for m in mine], axis=1)

    update_ref[...] = jnp.zeros_like(update_ref)
    held = (rhs_ref, low_ref, rest_ref, rest_low_ref)
    pair_updates(boxes_ref, list_ref, x_ref, q_ref, held, block_ref, update_ref, far_slot)
    for slot in range(2):
        to_before_ref[slot] = pltpu.roll(update_ref[slot], H * col, 1)
        to_after_ref[slot] = pltpu.roll(update_ref[2 + slot], H * col, 1)


def own_updates(
    boxes_ref, shared0, shared1, shared2, shared3, x_ref, rhs_in, low_in, rest_in, rest_low_in,
    update_ref,
    list_ref, rhs_ref, low_ref, rest_ref, rest_low_ref, q_ref, sum_ref, block_ref, sems,
):
    held = (rhs_ref, low_ref, rest_ref, rest_low_ref)
    given = (rhs_in, low_in, rest_in, rest_low_in)
    copies = [
        [pltpu.make_async_copy(src.at[i], dst.at[i], sems.at[i, n]) for n, (src, dst) in enumerate(zip(given, held))]
        for i in range(NBR)
    ]
    for group in copies:
        for copy in group:
            copy.start()
    list_pairs(boxes_ref, list_ref, True)
    put_pivots(q_ref, (shared0, shared1, shared2, shared3))
    sum_ref[...] = jnp.zeros_like(sum_ref)

    def arrive(i):
        for copy in copies[i]:
            copy.wait()

    pair_updates(
        boxes_ref, list_ref, x_ref, q_ref, held, block_ref, sum_ref, lambda b, k: pair_step(boxes_ref, b, k)[1], arrive
    )
    for slot in range(2):
        update_ref[slot] = pltpu.roll(sum_ref[slot], H * lax.axis_index("col"), 1)


def on_device(
    box_points, proxy_directions, point_order, neighbour_boxes, neighbour_places, pivot_inverse
):
    count = lax.axis_size("box")
    forward = [(i, (i + 1) % count) for i in range(count)]
    backward = [((i + 1) % count, i) for i in range(count)]
    smem = pl.BlockSpec(memory_space=pltpu.SMEM)
    vmem = pl.BlockSpec(memory_space=pltpu.VMEM)
    own, mine = pl.pallas_call(
        gather_inputs,
        out_shape=[jax.ShapeDtypeStruct((NBOX, 4, 512), f32), jax.ShapeDtypeStruct((4, S), f32)],
        in_specs=[vmem] * 4,
        out_specs=[vmem] * 2,
        name="gather_inputs",
    )(box_points.transpose(1, 0, 2), proxy_directions, point_order, pivot_inverse)
    before = lax.ppermute(own, "box", forward)
    after = lax.ppermute(own, "box", backward)
    cols = lax.axis_size("col")
    shared = [mine] + [
        lax.ppermute(mine, "col", [(i, (i + shift) % cols) for i in range(cols)]) for shift in range(1, 4)
    ]
    hbm = pl.BlockSpec(memory_space=pl.ANY)
    params = pltpu.CompilerParams(vmem_limit_bytes=56 * 1024 * 1024)
    list_scratch = pltpu.SMEM((NBR,), jnp.int32)
    kept_shapes = ((NBR, 512, 512), (NBR, 512, 512), (NBR, S, 512), (NBR, S, 512))
    kept = [pltpu.VMEM(shape, bf16) for shape in kept_shapes]
    turns = [pltpu.VMEM(shape, bf16) for shape in ((512, 512), (S, 512), (512, 512), (S, 512))]
    z_shape = (NBOX, 4, 512, 2 * H)
    q_scratch = pltpu.VMEM((NBOX, 2, S, 128), f32)
    z, source, *held = pl.pallas_call(
        own_tiles,
        out_shape=[jax.ShapeDtypeStruct(z_shape, f32), jax.ShapeDtypeStruct((NBOX, 512, 48), bf16)]
        + [jax.ShapeDtypeStruct(shape, bf16) for shape in kept_shapes],
        in_specs=[smem, smem, vmem],
        out_specs=[vmem, vmem] + [hbm] * 4,
        scratch_shapes=[list_scratch, pltpu.VMEM((NBOX, 8, 512), f32)] + kept + turns + [pltpu.SemaphoreType.DMA((NBR, 4))],
        compiler_params=params,
        cost_estimate=pl.CostEstimate(flops=20_000_000_000, bytes_accessed=16_000_000, transcendentals=2_000_000),
        name="own_tiles",
    )(neighbour_boxes, neighbour_places, own)
    rows = jax.ShapeDtypeStruct((NBOX, 2 * H, S), f32)
    interpolation, x, to_before, to_after = pl.pallas_call(
        far_pairs,
        out_shape=[jax.ShapeDtypeStruct((NBOX, 2, H, S), f32), jax.ShapeDtypeStruct((NBOX, 512, 512), bf16), rows, rows],
        in_specs=[smem, smem] + [vmem] * 6 + [hbm, vmem],
        out_specs=[vmem] * 4,
        scratch_shapes=[list_scratch, pltpu.VMEM((4, 8, 512), f32)] + kept + turns
        + [pltpu.VMEM(z_shape, f32), q_scratch, pltpu.VMEM((4, 2 * H, S), f32), pltpu.VMEM((4, 48, S), bf16), pltpu.VMEM((2, 512, S), f32), pltpu.SemaphoreType.DMA],
        compiler_params=params,
        cost_estimate=pl.CostEstimate(flops=60_000_000_000, bytes_accessed=8_000_000, transcendentals=4_000_000),
        name="far_pairs",
    )(neighbour_boxes, neighbour_places, before, after, *shared, z, source)
    from_before = lax.ppermute(to_after, "box", forward)
    from_after = lax.ppermute(to_before, "box", backward)
    update = pl.pallas_call(
        own_updates,
        out_shape=rows,
        in_specs=[smem] + [vmem] * 5 + [hbm] * 4,
        out_specs=vmem,
        scratch_shapes=[list_scratch] + kept
        + [q_scratch, pltpu.VMEM((NBOX, 2 * H, S), f32), pltpu.VMEM((2, 512, S), f32), pltpu.SemaphoreType.DMA((NBR, 4))],
        compiler_params=params,
        cost_estimate=pl.CostEstimate(flops=10_000_000_000, bytes_accessed=16_000_000, transcendentals=0),
        name="own_updates",
    )(neighbour_boxes, *shared, x, *held)
    return interpolation.transpose(0, 1, 3, 2), (update + from_before + from_after).reshape(NBOX, 2, H, S)


def solution(mesh):
    placed = (
        P("box", None, None),
        P(None, "col"),
        P("box", None),
        P("box", None),
        P("box", None),
        P("box", None, "col"),
    )
    return jax.shard_map(
        on_device,
        mesh=mesh,
        in_specs=placed,
        out_specs=(P("box", None, None, "col"), P("box", None, "col", None)),
        check_vma=False,
    )
```

```python
import math

import jax
import jax.numpy as jnp
import numpy as np
from jax import lax
from jax.experimental import pallas as pl
from jax.experimental.pallas import tpu as pltpu
from jax.sharding import PartitionSpec as P

S = 256
H = 64
NBR = 8
NBOX = 2
f32 = jnp.float32
bf16 = jnp.bfloat16
softening = 0.05
ridge_share = 0.05


def chebyshev_fit(function, count):
    nodes = 0.125 + 0.125 * np.cos(np.pi * (np.arange(256) + 0.5) / 256)
    fit = np.polynomial.chebyshev.Chebyshev.fit(nodes, function(np.sqrt(nodes)), count - 1, domain=[0, 0.25])
    return [float(c) for c in fit.convert(kind=np.polynomial.Polynomial).coef]


SIN_COEF = chebyshev_fit(lambda g: np.sin(np.pi * g) / (g * math.sqrt(math.pi)), 4)
COS_COEF = chebyshev_fit(lambda g: np.cos(np.pi * g) / math.sqrt(math.pi), 5)


def horner(z, coef):
    out = coef[-1]
    for c in coef[-2::-1]:
        out = out * z + c
    return out


def split2(x):
    high = x.astype(bf16)
    return high, (x - high.astype(f32)).astype(bf16)


def split3(x):
    high = x.astype(bf16).astype(f32)
    rest = x - high
    middle = rest.astype(bf16).astype(f32)
    return high, middle, (rest - middle).astype(bf16).astype(f32)


def dot(a, b, rhs_transposed=False, precision=None):
    dims = (((1,), (1 if rhs_transposed else 0,)), ((), ()))
    return lax.dot_general(a, b, dims, precision=precision, preferred_element_type=f32)


def turned(x):
    swapped = pltpu.roll(x, x.shape[1] // 2, 1)
    lane = lax.broadcasted_iota(jnp.int32, x.shape, 1)
    return jnp.where(lane < x.shape[1] // 2, -swapped, swapped)


def expand(x):
    return jnp.concatenate([x, turned(x)], axis=0)


def evaluate(v):
    inv = lax.rsqrt(v)
    turns = v * inv
    g = turns - jnp.round(turns)
    z = g * g
    s = g * horner(z, SIN_COEF)
    c = horner(z, COS_COEF)
    return inv * (1.0 / (2.0 * math.pi) - s * s), inv * (s * c)


def times(a, b):
    return a[0] * b[0] - a[1] * b[1], a[0] * b[1] + a[1] * b[0]


def invert(w):
    shape = (8, 2 * H)
    row_id = lax.broadcasted_iota(jnp.int32, shape, 0)
    lane_id = lax.broadcasted_iota(jnp.int32, shape, 1)
    line_id = lax.broadcasted_iota(jnp.int32, (1, 2 * H), 1)
    groups = [w[8 * g : 8 * g + 8] for g in range(H // 8)]
    for p in range(H // 8):
        columns = [
            [
                tuple(jnp.broadcast_to(w_g[:, at : at + 1], shape) for at in (8 * p + j, H + 8 * p + j))
                for j in range(8)
            ]
            for w_g in groups
        ]
        rows = groups[p]
        rows_t = turned(rows)
        small = list(columns[p])
        for j in range(8):
            at = 8 * p + j
            pivot = 1.0 / small[j][0][j : j + 1]
            row = jnp.where(line_id == at, pivot, jnp.where(line_id == H + at, 0.0, rows[j : j + 1] * pivot))
            row_t = jnp.where(line_id == H + at, pivot, jnp.where(line_id == at, 0.0, rows_t[j : j + 1] * pivot))
            here = row_id == j
            re = jnp.where(here, -1.0, small[j][0])
            im = jnp.where(here, 0.0, small[j][1])
            out = here | (lane_id == at) | (lane_id == H + at)
            rows = jnp.where(out, 0.0, rows) - re * row - im * row_t
            rows_t = jnp.where(out, 0.0, rows_t) - re * row_t + im * row
            for l in range(j + 1, 8):
                factor = tuple(x[j : j + 1] * pivot for x in small[l])
                step = times((re, im), factor)
                small[l] = tuple(jnp.where(here, 0.0, x) - y for x, y in zip(small[l], step))
        panel = ((lane_id >= 8 * p) & (lane_id < 8 * p + 8)) | ((lane_id >= H + 8 * p) & (lane_id < H + 8 * p + 8))
        for g in range(H // 8):
            if g == p:
                groups[g] = rows
                continue
            terms = [
                columns[g][j][0] * rows[j : j + 1] + columns[g][j][1] * rows_t[j : j + 1] for j in range(8)
            ]
            while len(terms) > 1:
                terms = [x + y for x, y in zip(terms[::2], terms[1::2])]
            groups[g] = jnp.where(panel, 0.0, groups[g]) - terms[0]
    return jnp.concatenate(groups, axis=0)


def on_diagonals(shape):
    return lax.broadcasted_iota(jnp.int32, shape, 0) == lax.broadcasted_iota(jnp.int32, shape, 1)


def row_ids(width):
    return lax.broadcasted_iota(jnp.int32, (8, width), 0)


def ordered(data):
    pick = (lax.broadcasted_iota(jnp.int32, (512, 512), 0).astype(f32) == data[3:4]).astype(bf16)
    parts = split3(2.0 * data - 1.0)
    got = dot(jnp.concatenate(parts + (jnp.zeros_like(data),), axis=0).astype(bf16), pick)
    points = jnp.where(row_ids(512)[:4] < 3, (got[0:4] + got[4:8]) + got[8:12], 0.0)
    return jnp.concatenate([points, jnp.zeros_like(points)], axis=0)


def features(points, is_source):
    rows = row_ids(points.shape[1])
    square = jnp.sum(points * points, axis=0, keepdims=True)
    if is_source:
        square = square + 4.0 * softening * softening
        high, middle, low = split3(points)
        groups = (high, high, middle, high, low, middle)
    else:
        high, middle, low = split3(-2.0 * points)
        groups = (high, middle, high, low, high, middle)
    own_row, other_row = (4, 3) if is_source else (3, 4)
    squares = split3(square)
    out = [
        jnp.where(rows == own_row, squares[i], jnp.where(rows == other_row, 1.0, group)) if i < 3 else group
        for i, group in enumerate(groups)
    ]
    return jnp.concatenate(out, axis=0)


def pair_step(boxes_ref, b, k):
    me, total = lax.axis_index("box"), lax.axis_size("box")
    box = boxes_ref[b, k]
    return lax.rem((box >> 1) - me + 1 + total, total), box & 1


def list_pairs(boxes_ref, list_ref, own):
    found = jnp.int32(0)
    for p in range(NBOX * NBR):
        step, _ = pair_step(boxes_ref, p // NBR, p % NBR)
        fits = (step == 1) if own else (step != 1)

        @pl.when(fits & (found < NBR))
        def _():
            list_ref[found] = p

        found = found + fits.astype(jnp.int32)


def pair_features(places_ref, points, b, k):
    code = places_ref[b, k]
    code = code + (code >= 13).astype(jnp.int32)
    rows = row_ids(512)
    move = jnp.zeros((8, 512), f32)
    for axis, digit in enumerate((code // 9, code // 3 % 3, code % 3)):
        move = jnp.where(rows == axis, (2 * digit - 2).astype(f32), move)
    got = features(points + move, False)
    back = lax.rem(S - H * lax.axis_index("col"), S)
    return pltpu.roll(got[:, :S], back, 1).astype(bf16), got[:, S:].astype(bf16)


def gram_piece(z_ref, b, in_refs, piece):
    main_ref, side_ref = in_refs
    half, n0 = piece
    if half == 0:
        left = jnp.concatenate([main_ref[2 * H * g : 2 * H * g + H] for g in range(4)], axis=0)
    else:
        left = side_ref[...]
    got = dot(left, main_ref[n0 : n0 + S], rhs_transposed=True)
    for i in range(2):
        z_ref[b, n0 // 128 + i, S * half : S * (half + 1)] += got[:, 2 * H * i : 2 * H * (i + 1)]


PIECES = {0: (0, 0), 2: (1, 0), 4: (0, S), 6: (1, S)}


def tile(source_ref, b, features_t, out_refs, kept, z_ref, b_in, in_refs):
    main_ref, side_ref = out_refs
    for g in range(8):
        if g in PIECES:
            gram_piece(z_ref, b_in, in_refs, PIECES[g])
        re, im = evaluate(dot(source_ref[b, g * H : (g + 1) * H], features_t))
        re_high, im_high = re.astype(bf16), im.astype(bf16)
        high = jnp.concatenate([re_high, im_high], axis=1)
        if g < 4:
            span = slice(2 * H * g, 2 * H * (g + 1))
            high = jnp.concatenate([high, jnp.concatenate([-im_high, re_high], axis=1)], axis=0)
            main_ref[span] = high
        else:
            span = slice(H * (g - 4), H * (g - 3))
            side_ref[span] = high
        if kept is None:
            continue
        i, rhs_ref, low_ref, rest_ref, rest_low_ref = kept
        re_low = (re - re_high.astype(f32)).astype(bf16)
        im_low = (im - im_high.astype(f32)).astype(bf16)
        low = jnp.concatenate([re_low, im_low], axis=1)
        if g < 4:
            low = jnp.concatenate([low, jnp.concatenate([-im_low, re_low], axis=1)], axis=0)
            rhs_ref[i, span] = high
            low_ref[i, span] = low
        else:
            rest_ref[i, span] = high
            rest_low_ref[i, span] = low


def pair_tiles(boxes_ref, places_ref, list_ref, source_ref, points_of, kept, z_ref, even, odd, after_each=None):
    for ref in odd:
        ref[...] = jnp.zeros_like(ref)

    @pl.loop(0, NBR)
    def _(i):
        p = list_ref[i]
        b_last = list_ref[jnp.maximum(i - 1, 0)] >> 3
        b, k = p >> 3, p & 7
        skeleton, redundant = pair_features(places_ref, points_of(b, k), b, k)
        tile(source_ref, b, skeleton, even, (i,) + kept, z_ref, b_last, odd)
        if after_each is not None:
            after_each(i)
        tile(source_ref, b, redundant, odd, None, z_ref, b, even)


def put_pivots(q_ref, shared):
    col = lax.axis_index("col")
    flat = jnp.concatenate([ref[3:4] for ref in shared] + [jnp.zeros((4, S), f32)], axis=0).T
    for b in range(NBOX):
        for part in range(2):
            first = (2 * b + part) * H
            for shift in range(4):
                rows = pl.ds(pl.multiple_of(lax.rem(col - shift + 4, 4) * H, H), H)
                q_ref[b, part, rows] = jnp.broadcast_to(flat[first : first + H, shift : shift + 1], (H, 128))


def pair_updates(boxes_ref, list_ref, x_ref, q_ref, held, block_ref, sum_ref, place_of, before_each=None):
    rhs_ref, low_ref, rest_ref, rest_low_ref = held

    def block_half(i, part):
        b = list_ref[i] >> 3
        lanes = slice(S * part, S * (part + 1))
        x_both = x_ref[b]
        both = dot(x_both, rhs_ref[i, :, lanes])
        rest = rest_ref[i, :, lanes].astype(f32) + rest_low_ref[i, :, lanes].astype(f32)
        block_ref[i % 2, S * part : S * (part + 1)] = rest - (
            (both[:S] + both[S:]) + dot(x_both[:S], low_ref[i, :, lanes])
        )

    def weigh(i):
        b = list_ref[i] >> 3
        first = jnp.concatenate([block_ref[i % 2, :S, :H], block_ref[i % 2, S:, :H]], axis=1)
        weighted = (q_ref[b, 0] * first + q_ref[b, 1] * turned(first)).T
        left = jnp.concatenate([weighted, jnp.concatenate([-weighted[H:], weighted[:H]], axis=0)], axis=1)
        return split2(left)

    def finish(i, left):
        high, low = left
        right_high, right_low = split2(block_ref[i % 2])
        got = dot(jnp.concatenate([high, low], axis=0), right_high)
        p = list_ref[i]
        sum_ref[place_of(p >> 3, p & 7)] -= (got[: 2 * H] + got[2 * H :]) + dot(high, right_low)

    for i in range(NBR + 1):
        if i < NBR:
            if before_each is not None:
                before_each(i)
            block_half(i, 0)
        if i > 0:
            left = weigh(i - 1)
        if i < NBR:
            block_half(i, 1)
        if i > 0:
            finish(i - 1, left)


def put_x(x_ref, x, b):
    high, low = split2(x)
    x_ref[b, :S] = high
    x_ref[b, S:] = low


def gather_inputs(points_ref, directions_ref, order_ref, pivot_ref, own_ref, mine_ref):
    for b in range(NBOX):
        for axis in range(3):
            own_ref[b, axis : axis + 1] = points_ref[axis, b : b + 1]
        own_ref[b, 3:4] = order_ref[b : b + 1].astype(f32)
        for part in range(2):
            first = (2 * b + part) * H
            mine_ref[3:4, first : first + H] = pivot_ref[b, part : part + 1]
    mine_ref[0:3] = directions_ref[...]


def own_tiles(
    boxes_ref, places_ref, own_ref,
    z_ref, source_ref, rhs_out, low_out, rest_out, rest_low_out,
    list_ref, point_ref, rhs_ref, low_ref, rest_ref, rest_low_ref, main0_ref, side0_ref, main1_ref, side1_ref, sems,
):
    list_pairs(boxes_ref, list_ref, True)
    for b in range(NBOX):
        point_ref[b] = ordered(own_ref[b])
        source_ref[b] = features(point_ref[b], True).T.astype(bf16)
    z_ref[...] = jnp.zeros_like(z_ref)
    even, odd = (main0_ref, side0_ref), (main1_ref, side1_ref)
    kept = (rhs_ref, low_ref, rest_ref, rest_low_ref)
    outs = (rhs_out, low_out, rest_out, rest_low_out)

    def copies(i):
        return [pltpu.make_async_copy(src.at[i], dst.at[i], sems.at[i, n]) for n, (src, dst) in enumerate(zip(kept, outs))]

    def start(i):
        for copy in copies(i):
            copy.start()

    pair_tiles(
        boxes_ref, places_ref, list_ref, source_ref,
        lambda b, k: point_ref[pair_step(boxes_ref, b, k)[1]],
        kept, z_ref, even, odd, start,
    )
    for piece in PIECES.values():
        gram_piece(z_ref, list_ref[NBR - 1] >> 3, odd, piece)
    for i in range(NBR):
        for copy in copies(i):
            copy.wait()


def solve(z_ref):
    highest = lax.Precision.HIGHEST
    on_diagonal = on_diagonals((H, 2 * H))
    for b in range(NBOX):
        total = jnp.zeros((H, 2 * H), f32)
        for c in range(4):
            total = total + jnp.where(on_diagonal, z_ref[b, c, c * H : (c + 1) * H], 0.0)
        trace = jnp.sum(jnp.sum(total, axis=0, keepdims=True), axis=1, keepdims=True)
        ridge = jnp.where(on_diagonal, ridge_share * trace / S, 0.0)
        for c in range(4):
            z_ref[b, c, c * H : (c + 1) * H] += ridge
    inverses = [invert(z_ref[b, 0, :H]) for b in range(NBOX)]
    for kb in range(4):
        rows = slice(kb * H, (kb + 1) * H)
        below = slice((kb + 1) * H, 512)
        following = slice((kb + 1) * H, (kb + 2) * H)
        spread = [expand(x) for x in inverses]
        blocks, others = [], []
        for b in range(NBOX):
            blocks.append(z_ref[b, kb, below])
            others.append({c: expand(z_ref[b, c, rows]) for c in range(4) if c != kb})
        if kb < 3:
            inverses = []
            for b in range(NBOX):
                top = dot(blocks[b][:H], spread[b], precision=highest)
                inverses.append(
                    invert(z_ref[b, kb + 1, following] - dot(top, others[b][kb + 1], precision=highest))
                )
        for b in range(NBOX):
            block = dot(blocks[b], spread[b], precision=highest)
            z_ref[b, kb, below] = block
            step = dot(block, jnp.concatenate(list(others[b].values()), axis=1), precision=highest)
            for i, c in enumerate(others[b]):
                z_ref[b, c, below] -= step[:, 2 * H * i : 2 * H * (i + 1)]


def far_pairs(
    boxes_ref, places_ref, before_ref, after_ref, shared0, shared1, shared2, shared3, z_in, source_ref,
    interp_ref, x_ref, to_before_ref, to_after_ref,
    list_ref, point_ref, rhs_ref, low_ref, rest_ref, rest_low_ref, main0_ref, side0_ref, main1_ref, side1_ref,
    z_ref, q_ref, update_ref, proxy_ref, block_ref,
):
    col = lax.axis_index("col")
    shared = (shared0, shared1, shared2, shared3)
    list_pairs(boxes_ref, list_ref, False)
    for slot in range(2):
        point_ref[slot] = ordered(before_ref[slot])
        point_ref[2 + slot] = ordered(after_ref[slot])
    for d in range(4):
        data = shared[d][...]
        points = jnp.concatenate([jnp.where(row_ids(S)[:4] < 3, 3.0 * data, 0.0), jnp.zeros_like(data)], axis=0)
        proxy_ref[d] = features(points, False).astype(bf16)
    put_pivots(q_ref, shared)
    z_ref[...] = z_in[...]
    even, odd = (main0_ref, side0_ref), (main1_ref, side1_ref)

    def far_slot(b, k):
        step, place = pair_step(boxes_ref, b, k)
        return (step & 2) + place

    pair_tiles(
        boxes_ref, places_ref, list_ref, source_ref, lambda b, k: point_ref[far_slot(b, k)],
        (rhs_ref, low_ref, rest_ref, rest_low_ref), z_ref, even, odd,
    )

    @pl.loop(0, 4)
    def _(i):
        b = i >> 1
        b_last = jnp.where(i == 0, list_ref[NBR - 1] >> 3, (i - 1) >> 1)
        d = 2 * (i & 1)
        tile(source_ref, b, proxy_ref[d], even, None, z_ref, b_last, odd)
        tile(source_ref, b, proxy_ref[d + 1], odd, None, z_ref, b, even)

    for piece in PIECES.values():
        gram_piece(z_ref, 1, odd, piece)
    solve(z_ref)
    for b in range(NBOX):
        x = jnp.concatenate([z_ref[b, c, S:] for c in range(4)], axis=1)
        put_x(x_ref, x, b)
        mine = [z_ref[b, c, pl.ds(pl.multiple_of(S + col * H, H), H)] for c in range(4)]
        for part in range(2):
            interp_ref[b, part] = jnp.concatenate([m[:, part * H : (part + 1) * H] for m in mine], axis=1)

    update_ref[...] = jnp.zeros_like(update_ref)
    held = (rhs_ref, low_ref, rest_ref, rest_low_ref)
    pair_updates(boxes_ref, list_ref, x_ref, q_ref, held, block_ref, update_ref, far_slot)
    for slot in range(2):
        to_before_ref[slot] = pltpu.roll(update_ref[slot], H * col, 1)
        to_after_ref[slot] = pltpu.roll(update_ref[2 + slot], H * col, 1)


def own_updates(
    boxes_ref, shared0, shared1, shared2, shared3, x_ref, rhs_in, low_in, rest_in, rest_low_in,
    update_ref,
    list_ref, rhs_ref, low_ref, rest_ref, rest_low_ref, q_ref, sum_ref, block_ref, sems,
):
    held = (rhs_ref, low_ref, rest_ref, rest_low_ref)
    given = (rhs_in, low_in, rest_in, rest_low_in)
    copies = [
        [pltpu.make_async_copy(src.at[i], dst.at[i], sems.at[i, n]) for n, (src, dst) in enumerate(zip(given, held))]
        for i in range(NBR)
    ]
    for group in copies:
        for copy in group:
            copy.start()
    list_pairs(boxes_ref, list_ref, True)
    put_pivots(q_ref, (shared0, shared1, shared2, shared3))
    sum_ref[...] = jnp.zeros_like(sum_ref)

    def arrive(i):
        for copy in copies[i]:
            copy.wait()

    pair_updates(
        boxes_ref, list_ref, x_ref, q_ref, held, block_ref, sum_ref, lambda b, k: pair_step(boxes_ref, b, k)[1], arrive
    )
    for slot in range(2):
        update_ref[slot] = pltpu.roll(sum_ref[slot], H * lax.axis_index("col"), 1)


def on_device(
    box_points, proxy_directions, point_order, neighbour_boxes, neighbour_places, pivot_inverse
):
    count = lax.axis_size("box")
    forward = [(i, (i + 1) % count) for i in range(count)]
    backward = [((i + 1) % count, i) for i in range(count)]
    smem = pl.BlockSpec(memory_space=pltpu.SMEM)
    vmem = pl.BlockSpec(memory_space=pltpu.VMEM)
    own, mine = pl.pallas_call(
        gather_inputs,
        out_shape=[jax.ShapeDtypeStruct((NBOX, 4, 512), f32), jax.ShapeDtypeStruct((4, S), f32)],
        in_specs=[vmem] * 4,
        out_specs=[vmem] * 2,
        name="gather_inputs",
    )(box_points.transpose(1, 0, 2), proxy_directions, point_order, pivot_inverse)
    before = lax.ppermute(own, "box", forward)
    after = lax.ppermute(own, "box", backward)
    cols = lax.axis_size("col")
    shared = [mine] + [
        lax.ppermute(mine, "col", [(i, (i + shift) % cols) for i in range(cols)]) for shift in range(1, 4)
    ]
    hbm = pl.BlockSpec(memory_space=pl.ANY)
    params = pltpu.CompilerParams(vmem_limit_bytes=56 * 1024 * 1024)
    list_scratch = pltpu.SMEM((NBR,), jnp.int32)
    kept_shapes = ((NBR, 512, 512), (NBR, 512, 512), (NBR, S, 512), (NBR, S, 512))
    kept = [pltpu.VMEM(shape, bf16) for shape in kept_shapes]
    turns = [pltpu.VMEM(shape, bf16) for shape in ((512, 512), (S, 512), (512, 512), (S, 512))]
    z_shape = (NBOX, 4, 512, 2 * H)
    q_scratch = pltpu.VMEM((NBOX, 2, S, 128), f32)
    z, source, *held = pl.pallas_call(
        own_tiles,
        out_shape=[jax.ShapeDtypeStruct(z_shape, f32), jax.ShapeDtypeStruct((NBOX, 512, 48), bf16)]
        + [jax.ShapeDtypeStruct(shape, bf16) for shape in kept_shapes],
        in_specs=[smem, smem, vmem],
        out_specs=[vmem, vmem] + [hbm] * 4,
        scratch_shapes=[list_scratch, pltpu.VMEM((NBOX, 8, 512), f32)] + kept + turns + [pltpu.SemaphoreType.DMA((NBR, 4))],
        compiler_params=params,
        cost_estimate=pl.CostEstimate(flops=20_000_000_000, bytes_accessed=16_000_000, transcendentals=2_000_000),
        name="own_tiles",
    )(neighbour_boxes, neighbour_places, own)
    rows = jax.ShapeDtypeStruct((NBOX, 2 * H, S), f32)
    interpolation, x, to_before, to_after = pl.pallas_call(
        far_pairs,
        out_shape=[jax.ShapeDtypeStruct((NBOX, 2, H, S), f32), jax.ShapeDtypeStruct((NBOX, 512, 512), bf16), rows, rows],
        in_specs=[smem, smem] + [vmem] * 8,
        out_specs=[vmem] * 4,
        scratch_shapes=[list_scratch, pltpu.VMEM((4, 8, 512), f32)] + kept + turns
        + [pltpu.VMEM(z_shape, f32), q_scratch, pltpu.VMEM((4, 2 * H, S), f32), pltpu.VMEM((4, 48, S), bf16), pltpu.VMEM((2, 512, S), f32)],
        compiler_params=params,
        cost_estimate=pl.CostEstimate(flops=60_000_000_000, bytes_accessed=8_000_000, transcendentals=4_000_000),
        name="far_pairs",
    )(neighbour_boxes, neighbour_places, before, after, *shared, z, source)
    from_before = lax.ppermute(to_after, "box", forward)
    from_after = lax.ppermute(to_before, "box", backward)
    update = pl.pallas_call(
        own_updates,
        out_shape=rows,
        in_specs=[smem] + [vmem] * 5 + [hbm] * 4,
        out_specs=vmem,
        scratch_shapes=[list_scratch] + kept
        + [q_scratch, pltpu.VMEM((NBOX, 2 * H, S), f32), pltpu.VMEM((2, 512, S), f32), pltpu.SemaphoreType.DMA((NBR, 4))],
        compiler_params=params,
        cost_estimate=pl.CostEstimate(flops=10_000_000_000, bytes_accessed=16_000_000, transcendentals=0),
        name="own_updates",
    )(neighbour_boxes, *shared, x, *held)
    return interpolation.transpose(0, 1, 3, 2), (update + from_before + from_after).reshape(NBOX, 2, H, S)


def solution(mesh):
    placed = (
        P("box", None, None),
        P(None, "col"),
        P("box", None),
        P("box", None),
        P("box", None),
        P("box", None, "col"),
    )
    return jax.shard_map(
        on_device,
        mesh=mesh,
        in_specs=placed,
        out_specs=(P("box", None, None, "col"), P("box", None, "col", None)),
        check_vma=False,
    )
```
